32 devices in a mesh: row: 4 (over z), col: 8 (over y, x, core).
Axes of the slice: x: 2, y: 2, z: 4, core: 2. Of those that a mesh axis runs over, the one named last changes fastest.
Arguments:
- coeffs: float32 [512, 3, 64, 128], P(('row', 'col')), may hold values from -0.18 to 0.18
- degree: int32 [512], P(('row', 'col')), may hold values from 16 to 63
- material: float32 [512, 2], P(('row', 'col')), may hold values from 0.2 to 2
- split_coeffs: float32 [128, 3, 64, 64], P(('row', 'col')), may hold values from -0.18 to 0.18
- split_material: float32 [64, 2], replicated, may hold values from 0.2 to 2
- separation: float32 [3, 512, 8], P(None, ('row', 'col')), may hold values from -2.6 to 2.6, as said below
- reader_dev: int32 [512, 8], P(('row', 'col')), may hold values from 0 to 31, all different within a row; in each aligned block of 16 rows (0 to 15, 16 to 31, ...) at most 6 rows name the same one
- reader_slot: int32 [512, 8], P(('row', 'col')), may hold values from 0 to 15
Outputs:
- traction_coeffs: float32 [512, 64, 128], P(('row', 'col'))
- split_traction: float32 [128, 64, 64], P(('row', 'col'))
- near_velocity: float32 [3, 2048], P(None, ('row', 'col'))
The draws below stay inside these ranges and needn't reach their ends.
Inputs may be any that keep to these rules, and one draw needn't show every extreme that they name: `reader_dev`: each ordinary drop names 8 different devices; among the drops of one device at most 6 name the same device, and some device is named exactly 6 times. Each entry's separation vector has a length between 1.9 and 2.6.
All inputs are finite; a program needn't handle non-finite values.
Results may differ from the reference program's by a relative error of at most 0.019.
Values may be sent and summed in bfloat16 or wider, within the bound.
A program may use at most 128 MiB of HBM per device.

```python
import math
import jax
import jax.numpy as jnp
import numpy as np
from jax import lax

L = 64
MH = 32
NLAT = 64
NLON = 128
TPTS = 4
DROPS_DEV = 16
SPLIT_DEV = 4
READERS = 8
CAP = 6
DROPS = 512
SPLIT_HALVES = 128
SPLIT_PAIRS = 64
N_ROW = 4
N_COL = 8
DEVICES = 32


def draw_separation(key, part):
    key_polar = jax.random.fold_in(key, 11)
    key_azimuth = jax.random.fold_in(key, 23)
    key_length = jax.random.fold_in(key, 37)
    cosine = jax.random.uniform(key_polar, (DROPS, READERS), jnp.float32, -1.0, 1.0)
    azimuth = jax.random.uniform(key_azimuth, (DROPS, READERS), jnp.float32, 0.0, 2.0 * math.pi)
    unit = jax.random.uniform(key_length, (DROPS, READERS), jnp.float32, 0.0, 1.0)
    length = 2.0 + 0.6 * unit
    planar = jnp.sqrt(jnp.maximum(1.0 - cosine * cosine, 0.0))
    return jnp.stack([length * planar * jnp.cos(azimuth), length * planar * jnp.sin(azimuth), length * cosine], axis=0)


def set_ends(values, stream_key, smallest, largest):
    dims = values.shape
    place = [jax.random.randint(jax.random.fold_in(stream_key, axis), (), 0, dims[axis]) for axis in range(len(dims))]
    values = values.at[tuple(place)].set(smallest)
    longest = dims.index(max(dims))
    place[longest] = (place[longest] + 1) % dims[longest]
    return values.at[tuple(place)].set(largest)


def level_of(own_key, shape, pieces, smallest, high):
    def one(dim, shards_of):
        draws = jax.random.uniform(jax.random.fold_in(jax.random.fold_in(own_key, 6), dim), (shards_of,), jnp.float32, smallest / len(pieces), high / len(pieces))
        return jnp.repeat(jnp.exp(draws), shape[dim] // shards_of).reshape((-1,) + (1,) * (len(shape) - dim - 1))

    factor_of = one(*pieces[0])
    for cut in pieces[1:]:
        factor_of = factor_of * one(*cut)
    return factor_of


def assign_block(key, own, number, rows, count, top, bound, lean):
    sequence = jax.random.permutation(key, count)
    crowded, usual = shares(count, rows * top, bound, lean, True), shares(count, rows * top, bound, lean, False)
    places = jnp.arange(count)

    def named(sizes, rotation):
        used = int((sizes > 0).sum())
        fixed = max(1, used // 4)
        moved = fixed + (places - fixed + rotation * (used - fixed)) % max(1, count - fixed)
        return jnp.zeros((count,), jnp.int32).at[sequence[jnp.where(places < fixed, places, moved)]].set(jnp.asarray(sizes, jnp.int32))

    sizes = jnp.where(number % 4 == 0, named(crowded, number // 4), named(usual, number - number // 4 - 1))
    mixed = jax.random.permutation(jax.random.fold_in(own, 3), count)
    donor, sink = mixed[0:count // 2 * 2:2], mixed[1:count // 2 * 2:2]
    slack = jnp.minimum(sizes[donor] - 1, bound - sizes[sink]) // 2
    slack = jnp.where((donor == sequence[0]) | (sink == sequence[0]) | (sizes[sink] == 0), 0, jnp.maximum(slack, 0))
    moved = jax.random.randint(jax.random.fold_in(own, 4), (count // 2,), 0, 1 << 20) % (slack + 1)
    sizes = sizes.at[donor].add(-moved).at[sink].add(moved)
    items = jnp.searchsorted(jnp.cumsum(sizes), jnp.arange(rows * top), side="right").astype(jnp.int32)
    listing = items.reshape(top, rows).T
    listing = listing[jax.random.permutation(jax.random.fold_in(own, 1), rows)]
    rotation = jax.random.randint(jax.random.fold_in(own, 2), (rows, 1), 0, top)
    return jnp.take_along_axis(listing, (jnp.arange(top)[None, :] + rotation) % top, axis=1)


def shares(amount, total, most, skew, full):
    weights = [(1 << 20) // math.isqrt(grade ** skew) + 1 for grade in range(1, amount + 1)]
    largest = most if full else min(most, max(-(-total // amount), total * weights[0] // sum(weights)))
    least = 1 if total - largest >= amount - 1 else 0
    holding, spare = [largest] + [least] * (amount - 1), total - largest - least * (amount - 1)
    while spare > 0:
        movable = [i for i in range(1, amount) if holding[i] < largest] or [i for i in range(1, amount) if holding[i] < most]
        mass, budget = sum([weights[i] for i in movable]), spare
        for i in movable:
            addition = min(most - holding[i], max(1, budget * weights[i] // mass), spare)
            holding[i] = holding[i] + addition
            spare = spare - addition
    return np.array(holding)


def centred(own_key, extent, spread, limit, split=(), kind=jnp.bfloat16):
    values = jax.random.normal(own_key, extent, jnp.float32) * spread
    if len(split) > 0:
        values = level_of(own_key, extent, split, -0.22, 0.18) * values
    return jnp.clip(values, min=-limit, max=limit).astype(kind)


def setup_inputs(seed: int = 0) -> dict:
    arg_keys = jax.random.split(jax.random.key(seed), 9)
    coeffs = centred(arg_keys[0], (DROPS, 3, L, 2 * L), 0.03, 0.18, ((0, 32),), jnp.float32)
    degree = set_ends(jax.random.randint(arg_keys[1], (DROPS,), L // 4, L), jax.random.fold_in(arg_keys[1], 1), L // 4, L - 1).astype(jnp.int32)
    material = jnp.clip(jnp.exp(math.log(2.0) - 2.3025851 * jax.random.uniform(arg_keys[2], (DROPS, 2), jnp.float32) ** level_of(arg_keys[2], (DROPS, 2), ((0, 32),), -0.2, 0.2)), 0.2, 2.0)
    split_coeffs = centred(arg_keys[3], (SPLIT_HALVES, 3, L, L), 0.03, 0.18, ((0, 32),), jnp.float32)
    split_material = jnp.clip(jnp.exp(jax.random.uniform(arg_keys[4], (SPLIT_PAIRS, 2), jnp.float32, math.log(0.2), math.log(2.0))), 0.2, 2.0)
    separation = draw_separation(jax.random.fold_in(arg_keys[8], 71), 0)
    reader_dev_keys = jax.random.split(jax.random.fold_in(arg_keys[6], 1), DROPS // DROPS_DEV)
    reader_dev_turns = jax.random.permutation(jax.random.fold_in(arg_keys[6], 3), DROPS // DROPS_DEV)
    reader_dev = jax.vmap(lambda own, number: assign_block(jax.random.fold_in(arg_keys[6], 2), own, number, DROPS_DEV, DEVICES, READERS, CAP, 2))(reader_dev_keys, reader_dev_turns).reshape((DROPS, READERS))
    reader_slot = set_ends(jax.random.randint(arg_keys[7], (DROPS, READERS), 0, DROPS_DEV), jax.random.fold_in(arg_keys[7], 1), 0, DROPS_DEV - 1).astype(jnp.int32)
    return {"coeffs": coeffs, "degree": degree, "material": material, "split_coeffs": split_coeffs, "split_material": split_material, "separation": separation, "reader_dev": reader_dev, "reader_slot": reader_slot}


HIGH = lax.Precision.HIGHEST
SOFTENING = 0.04

def spectral_tables(degrees):
    nlat = degrees
    nlon = 2 * degrees
    theta_lat = (np.arange(nlat) + 0.5) * (math.pi / nlat)
    cosine = np.cos(theta_lat)
    sine_theta = np.sin(theta_lat)
    legendre = np.zeros((degrees, nlat, degrees))
    for order in range(degrees):
        log_total = 0.0
        for step_index in range(1, order + 1):
            log_total = log_total + math.log((2.0 * step_index + 1.0) / (2.0 * step_index))
        diag_value = np.exp(0.5 * log_total + order * np.log(sine_theta)) / math.sqrt(4.0 * math.pi)
        legendre[order, :, order] = diag_value
        prev_two = diag_value
        if order + 1 < degrees:
            prev_one = math.sqrt(2.0 * order + 3.0) * cosine * diag_value
            legendre[order, :, order + 1] = prev_one
            for level in range(order + 2, degrees):
                alpha_term = math.sqrt((4.0 * level * level - 1.0) / (level * level - order * order))
                beta_term = math.sqrt(((level - 1.0) ** 2 - order * order) / (4.0 * (level - 1.0) ** 2 - 1.0))
                current = alpha_term * (cosine * prev_one - beta_term * prev_two)
                legendre[order, :, level] = current
                prev_two = prev_one
                prev_one = current
    order_index = np.arange(degrees)
    lon_index = np.arange(nlon)
    phase_angle = order_index[:, None] * lon_index[None, :] % nlon * (2.0 * math.pi / nlon)
    fourier = np.concatenate([np.cos(phase_angle), np.sin(phase_angle)], axis=0)
    quad_weight = sine_theta * (math.pi / nlat) * (2.0 * math.pi / nlon)
    longitude = lon_index * (2.0 * math.pi / nlon)
    normals = np.stack([sine_theta[:, None] * np.cos(longitude)[None, :], sine_theta[:, None] * np.sin(longitude)[None, :], cosine[:, None] * np.ones((1, nlon))], axis=0)
    return (jnp.asarray(legendre, dtype=jnp.float32), jnp.asarray(fourier, dtype=jnp.float32), jnp.asarray(quad_weight, dtype=jnp.float32), jnp.asarray(normals, dtype=jnp.float32))

def legendre_synth(coeff, legendre):
    batch_size, degrees, coef_width = coeff.shape
    orders = legendre.shape[0]
    parted = coeff.reshape(batch_size, degrees, 2, orders)
    return jnp.einsum('mjl,nlcm->njcm', legendre, parted, precision=HIGH)

def fourier_synth(partial_legendre, fourier_rows):
    batch_size, nlat, two, orders = partial_legendre.shape
    return jnp.einsum('njw,wk->njk', partial_legendre.reshape(batch_size, nlat, two * orders), fourier_rows, precision=HIGH)

def analysis_fourier(traction_grid, fourier, quad_weight):
    batch_size, nlat, nlon = traction_grid.shape
    projected = jnp.einsum('bjk,wk->bjw', traction_grid, fourier, precision=HIGH) * quad_weight[None, :, None]
    return projected.reshape(batch_size, nlat, 2, fourier.shape[0] // 2)

def analysis_legendre(coef_grid, legendre):
    batch_size = coef_grid.shape[0]
    result = jnp.einsum('mjl,bjcm->blcm', legendre, coef_grid, precision=HIGH)
    return result.reshape(batch_size, legendre.shape[2], 2 * legendre.shape[0])

def prepare(coeffs, keep_mask):
    degrees = coeffs.shape[2]
    degree_value = jnp.arange(degrees, dtype=jnp.float32)
    shape_part = coeffs[:, 0] * keep_mask
    curvature = shape_part * (degree_value * (degree_value + 1.0) / (degrees * degrees))[None, :, None]
    electric = 3.0 * coeffs[:, 1] * keep_mask
    viscous = 3.0 * coeffs[:, 2] * keep_mask * ((degree_value + 2.0) / degrees)[None, :, None]
    return jnp.stack([shape_part, curvature, electric, viscous], axis=1)

def traction(surface, material):
    radius = jnp.exp(surface[:, 0])
    traction_grid = material[:, 0, None, None] * surface[:, 1] + 0.5 * surface[:, 2] * surface[:, 2] + 2.0 * material[:, 1, None, None] * surface[:, 3]
    return (radius, traction_grid)

def drop_work(coeffs, keep_mask, material, legendre, fourier, quad_weight):
    batch_size, fields, degrees, coef_width = coeffs.shape
    prepared = prepare(coeffs, keep_mask)
    partial_legendre = legendre_synth(prepared.reshape(batch_size * 4, degrees, coef_width), legendre)
    surface = fourier_synth(partial_legendre, fourier)
    surface = surface.reshape(batch_size, 4, surface.shape[1], surface.shape[2])
    radius, traction_grid = traction(surface, material)
    result = analysis_legendre(analysis_fourier(traction_grid, fourier, quad_weight), legendre) * keep_mask
    return (result, radius, traction_grid)

def velocity_terms(radius, traction_grid, spacing, target_radius, cell_weight, cell_normal, target_normal):
    load_grid = traction_grid * radius * radius * cell_weight[None, :]
    target_point = spacing[:, :, None] + target_radius[None] * target_normal[:, None, :]
    surface_point = radius[None] * cell_normal[:, None, :]
    offset = target_point[:, :, :, None] - surface_point[:, :, None, :]
    distance_sq = lax.optimization_barrier(jnp.sum(offset * offset, axis=0))
    softened = distance_sq + SOFTENING
    weight = load_grid[:, None, :] / (softened * jnp.sqrt(softened))
    normal_dot = lax.optimization_barrier(jnp.sum(offset * cell_normal[:, None, None, :], axis=0))
    stokeslet = weight[None] * (cell_normal[:, None, None, :] * (distance_sq + 2.0 * SOFTENING)[None] + offset * normal_dot[None])
    return lax.optimization_barrier(jnp.sum(stokeslet, axis=3)) / (8.0 * math.pi)

def reference(coeffs, degree, material, split_coeffs, split_material, separation, reader_dev, reader_slot):
    legendre, fourier, quad_weight, normals = spectral_tables(L)
    degree_index = jnp.arange(L, dtype=jnp.int32)
    order_full = jnp.arange(2 * L, dtype=jnp.int32) % L
    order_mask = (degree_index[:, None] >= order_full[None, :]).astype(jnp.float32)

    def drop_block(block_args):
        block_coeffs, block_degree, block_material = block_args
        keep_mask = order_mask[None] * (degree_index[None, :, None] <= block_degree[:, None, None]).astype(jnp.float32)
        return drop_work(block_coeffs, keep_mask, block_material, legendre, fourier, quad_weight)
    result, radius, traction_grid = lax.map(drop_block, (coeffs.reshape(DEVICES, DROPS_DEV, 3, L, 2 * L), degree.reshape(DEVICES, DROPS_DEV), material.reshape(DEVICES, DROPS_DEV, 2)))
    traction_coeffs = result.reshape(DROPS, L, 2 * L)
    pair_view = split_coeffs.reshape(N_ROW // 2, 2, N_COL, SPLIT_DEV, 3, L, 2, MH)
    split_full = jnp.transpose(pair_view, (0, 2, 3, 4, 5, 6, 1, 7)).reshape(SPLIT_PAIRS, 3, L, 2 * L)
    split_result, split_radius, split_grid = drop_work(split_full, order_mask[None], split_material, legendre, fourier, quad_weight)
    split_back = split_result.reshape(N_ROW // 2, N_COL, SPLIT_DEV, L, 2, 2, MH)
    split_traction = jnp.transpose(split_back, (0, 5, 1, 2, 3, 4, 6)).reshape(SPLIT_HALVES, L, L)
    cell_count = NLAT * NLON
    cell_weight = jnp.broadcast_to(quad_weight[:, None], (NLAT, NLON)).reshape(cell_count)
    cell_normal = normals.reshape(3, cell_count)
    near_grid = jnp.stack([radius.reshape(DROPS, NLAT, NLON), traction_grid.reshape(DROPS, NLAT, NLON)], axis=1).astype(jnp.bfloat16)
    target_radius = near_grid[:, 0, NLAT // 4::NLAT // 2, ::NLON // 2].reshape(DROPS, TPTS)
    target_normal = normals[:, NLAT // 4::NLAT // 2, ::NLON // 2].reshape(3, TPTS)
    flat_grid = near_grid.reshape(DROPS, 2 * cell_count)
    sources = jnp.repeat(jnp.arange(DROPS, dtype=jnp.int32), READERS)
    targets = (reader_dev * DROPS_DEV + reader_slot).reshape(-1).astype(jnp.int32)
    pair_count = DROPS * READERS
    block_size = math.gcd(pair_count, 16)
    block_total = pair_count // block_size
    spacing_blocks = jnp.transpose(separation.reshape(3, block_total, block_size), (1, 0, 2))

    def near_block(block_args):
        block_source, block_target, block_spacing = block_args
        source_grid = flat_grid[block_source].astype(jnp.float32).reshape(block_size, 2, cell_count)
        return velocity_terms(source_grid[:, 0], source_grid[:, 1], block_spacing, target_radius[block_target].astype(jnp.float32), cell_weight, cell_normal, target_normal)
    velocity = lax.map(near_block, (sources.reshape(block_total, block_size), targets.reshape(block_total, block_size), spacing_blocks))
    velocity = jnp.transpose(velocity, (1, 0, 2, 3)).reshape(3, pair_count, TPTS)
    near_velocity = jnp.zeros((3, DROPS, TPTS), jnp.float32).at[:, targets].add(velocity).reshape(3, DROPS * TPTS)
    return (traction_coeffs, split_traction, near_velocity)
```

```python
import functools
import math

import jax
import jax.numpy as jnp
import numpy as np
from jax import lax
from jax.experimental import pallas as pl
from jax.experimental.pallas import tpu as pltpu
from jax.sharding import PartitionSpec as P

SOFTENING = 0.04
LANES = 128
F32 = jnp.float32
BF16 = jnp.bfloat16


def spectral_tables(degrees):
    nlon = 2 * degrees
    theta = (np.arange(degrees) + 0.5) * (math.pi / degrees)
    cosine, sine = np.cos(theta), np.sin(theta)
    legendre = np.zeros((degrees, degrees, degrees))
    for order in range(degrees):
        total = sum(math.log((2.0 * i + 1.0) / (2.0 * i)) for i in range(1, order + 1))
        older = np.exp(0.5 * total + order * np.log(sine)) / math.sqrt(4.0 * math.pi)
        legendre[order, :, order] = older
        if order + 1 < degrees:
            newer = math.sqrt(2.0 * order + 3.0) * cosine * older
            legendre[order, :, order + 1] = newer
            for l in range(order + 2, degrees):
                a = math.sqrt((4.0 * l * l - 1.0) / (l * l - order * order))
                b = math.sqrt(((l - 1.0) ** 2 - order * order) / (4.0 * (l - 1.0) ** 2 - 1.0))
                older, newer = newer, a * (cosine * newer - b * older)
                legendre[order, :, l] = newer
    phase = np.arange(degrees)[:, None] * np.arange(nlon)[None, :] % nlon * (2.0 * math.pi / nlon)
    fourier = np.concatenate([np.cos(phase), np.sin(phase)], axis=0)
    weight = sine * (math.pi / degrees) * (2.0 * math.pi / nlon)
    lon = np.arange(nlon) * (2.0 * math.pi / nlon)
    return legendre, fourier, weight, sine, cosine, lon


def parity_tables(legendre, weight):
    degrees = legendre.shape[0]
    half = degrees // 2
    order = np.arange(2 * degrees) % degrees
    by_lane = legendre[order]
    step = np.arange(half)
    even = np.zeros((half, half, 2 * degrees))
    odd = np.zeros((half, half, 2 * degrees))
    for lane, m in enumerate(order):
        even[:, :, lane] = by_lane[lane][:half, 2 * step + m % 2].T
        odd[:, :, lane] = by_lane[lane][:half, 2 * step + 1 - m % 2].T
    scale = weight[:half, None, None]
    back_even = np.transpose(even, (1, 0, 2)) * scale
    back_odd = np.transpose(odd, (1, 0, 2)) * scale
    return [np.asarray(t, np.float32) for t in (even, odd, back_even, back_odd)]


def spectral_kernel(
    degree_ref, material_ref, coeffs_ref, even_ref, odd_ref, back_even_ref, back_odd_ref,
    fourier_ref, project_ref, weight_ref, out_ref, radius_ref, load_ref,
    field_scr, part_scr, back_scr,
):
    count, fields, degrees, width = coeffs_ref.shape
    half = degrees // 2
    first = pl.program_id(0) * count
    level = lax.broadcasted_iota(jnp.int32, (degrees, width), 0)
    levelf = level.astype(F32)
    curve = levelf * (levelf + 1.0) * (1.0 / (degrees * degrees))
    viscous = (levelf + 2.0) * (6.0 / degrees)
    half_level = lax.broadcasted_iota(jnp.int32, (half, width), 0)
    even_order = lax.broadcasted_iota(jnp.int32, (half, width), 1) % 2 == 0

    def one_drop(d, carry):
        degree = degree_ref[first + d]
        tension = material_ref[2 * (first + d)]
        viscosity = material_ref[2 * (first + d) + 1]
        keep = level <= degree
        shape = jnp.where(keep, coeffs_ref[d, 0], 0.0)
        field_scr[0] = shape
        field_scr[1] = shape * (tension * curve) + jnp.where(
            keep, coeffs_ref[d, 2] * (viscosity * viscous), 0.0
        )
        field_scr[2] = jnp.where(keep, 3.0 * coeffs_ref[d, 1], 0.0)
        for f in range(3):
            low = field_scr[f, pl.ds(0, half, stride=2), :]
            high = field_scr[f, pl.ds(1, half, stride=2), :]
            part_scr[2 * f] = jnp.where(even_order, low, high)
            part_scr[2 * f + 1] = jnp.where(even_order, high, low)
        total = [jnp.zeros((half, width), F32) for _ in range(6)]
        for i in range(half):
            pe, po = even_ref[i], odd_ref[i]
            for f in range(3):
                total[2 * f] = total[2 * f] + pe * part_scr[2 * f, i : i + 1, :]
                total[2 * f + 1] = total[2 * f + 1] + po * part_scr[2 * f + 1, i : i + 1, :]
        rows = []
        for f in range(3):
            rows += [total[2 * f] + total[2 * f + 1], total[2 * f] - total[2 * f + 1]]
        rows = jnp.concatenate(rows, axis=0)
        coarse = rows.astype(BF16)
        fine = (rows - coarse.astype(F32)).astype(BF16)
        f_coarse, f_fine = fourier_ref[0], fourier_ref[1]
        surface = (
            jnp.dot(coarse, f_coarse, preferred_element_type=F32)
            + jnp.dot(fine, f_coarse, preferred_element_type=F32)
            + jnp.dot(coarse, f_fine, preferred_element_type=F32)
        )
        radius = jnp.exp(surface[:degrees])
        potential = surface[2 * degrees :]
        traction = surface[degrees : 2 * degrees] + 0.5 * potential * potential
        radius_ref[d] = radius
        load_ref[d] = traction * radius * radius * weight_ref[...]
        project = jnp.dot(traction.astype(BF16), project_ref[...], preferred_element_type=F32)
        back_scr[0] = project[:half] + project[half:]
        back_scr[1] = project[:half] - project[half:]
        low = jnp.zeros((half, width), F32)
        high = jnp.zeros((half, width), F32)
        for j in range(half):
            low = low + back_even_ref[j] * back_scr[0, j : j + 1, :]
            high = high + back_odd_ref[j] * back_scr[1, j : j + 1, :]
        out_ref[d, pl.ds(0, half, stride=2), :] = jnp.where(
            2 * half_level <= degree, jnp.where(even_order, low, high), 0.0
        )
        out_ref[d, pl.ds(1, half, stride=2), :] = jnp.where(
            2 * half_level + 1 <= degree, jnp.where(even_order, high, low), 0.0
        )
        return carry

    lax.fori_loop(0, count, one_drop, 0)


def spectral(coeffs, degree, material, tables):
    drops, fields, degrees, width = coeffs.shape
    legendre, fourier, weight, sine, cosine, lon = tables
    half = degrees // 2
    block = math.gcd(drops, 4)
    f32 = jnp.asarray(fourier, F32)
    coarse = f32.astype(BF16)
    fourier_parts = jnp.stack([coarse, (f32 - coarse.astype(F32)).astype(BF16)])
    project = jnp.asarray(fourier.T, BF16)
    folded = np.concatenate([weight[:half], weight[:half]]) / (8.0 * math.pi)
    weight_grid = jnp.asarray(np.broadcast_to(folded[:, None], (degrees, width)), F32)
    parity = [jnp.asarray(t) for t in parity_tables(legendre, weight)]
    whole = lambda a: pl.BlockSpec(a.shape, lambda i: (0,) * a.ndim)
    smem = pl.BlockSpec(memory_space=pltpu.SMEM)
    consts = parity + [fourier_parts, project, weight_grid]
    grid_spec = pl.BlockSpec((block, degrees, width), lambda i: (i, 0, 0))
    return pl.pallas_call(
        spectral_kernel,
        grid=(drops // block,),
        in_specs=[smem, smem, pl.BlockSpec((block, fields, degrees, width), lambda i: (i, 0, 0, 0))]
        + [whole(a) for a in consts],
        out_specs=[grid_spec] * 3,
        out_shape=[jax.ShapeDtypeStruct((drops, degrees, width), F32)] * 3,
        scratch_shapes=[
            pltpu.VMEM((3, degrees, width), F32),
            pltpu.VMEM((6, half, width), F32),
            pltpu.VMEM((2, half, width), F32),
        ],
        compiler_params=pltpu.CompilerParams(vmem_limit_bytes=32 << 20),
        cost_estimate=pl.CostEstimate(
            flops=drops * 5_000_000, bytes_accessed=drops * 300_000, transcendentals=drops * 8192
        ),
    )(degree, material.reshape(-1), coeffs, *consts)


def near_kernel(
    normals, index_ref, slot_ref, dest_ref, sep_ref, points_ref, radius_ref, load_ref,
    turn_ref, tilt_ref, out_ref, target_scr, spread_scr,
):
    drops, degrees, width = radius_ref.shape
    entries = index_ref.shape[0]
    readers = entries // drops
    half = degrees // 2
    targets = points_ref.shape[0]
    columns = spread_scr.shape[1]
    point_count = len(normals)
    pick = lax.broadcasted_iota(jnp.int32, (entries, targets), 1) == index_ref[...]
    target_scr[...] = jnp.dot(
        pick.astype(F32).astype(BF16), points_ref[...], preferred_element_type=F32
    )
    lane = lax.broadcasted_iota(jnp.int32, (readers, columns), 1)
    block = drops * point_count
    kind = lane // block * point_count + lane % point_count
    lane_slot = lane % block // point_count

    def one_drop(d, carry):
        rows = pl.ds(pl.multiple_of(d * readers, readers), readers)
        sep = sep_ref[rows, :]
        reach = target_scr[rows, :]
        xs, ring, height, square = [], [], [], []
        for p in range(point_count):
            at = reach[:, p : p + 1]
            x = [
                jnp.broadcast_to(sep[:, c : c + 1] + at * normals[p][c], (readers, width))
                for c in range(3)
            ]
            xs.append(x)
            ring.append(x[0] * turn_ref[0:1, :] + x[1] * turn_ref[1:2, :])
            height.append(x[2])
            square.append(x[0] * x[0] + x[1] * x[1] + x[2] * x[2] + SOFTENING)

        def cell(a, r, rr, h, sq):
            off = a - r
            m = r * off
            t = (sq - rr) - m
            rho = t - m
            inv = lax.rsqrt(rho)
            g = (inv * h) * (inv * inv)
            return g * ((rho - m) + SOFTENING), g * off

        def tile(jt, acc):
            acc = list(acc)
            base = pl.multiple_of(jt * 8, 8)
            for q in range(8):
                j = base + q
                r0 = radius_ref[d, pl.ds(j, 1), :]
                r1 = radius_ref[d, pl.ds(j + half, 1), :]
                h0 = load_ref[d, pl.ds(j, 1), :]
                h1 = load_ref[d, pl.ds(j + half, 1), :]
                s = tilt_ref[0, pl.ds(j, 1), :]
                c = tilt_ref[1, pl.ds(j, 1), :]
                q0, q1 = r0 * r0, r1 * r1
                for p in range(point_count):
                    flat = s * ring[p]
                    up = c * height[p]
                    w0, v0 = cell(flat + up, r0, q0, h0, square[p])
                    w1, v1 = cell(flat - up, r1, q1, h1, square[p])
                    acc[3 * p] = acc[3 * p] + s * (w0 + w1)
                    acc[3 * p + 1] = acc[3 * p + 1] + c * (w0 - w1)
                    acc[3 * p + 2] = acc[3 * p + 2] + (v0 + v1)
            return tuple(acc)

        zero = jnp.zeros((readers, width), F32)
        acc = lax.fori_loop(0, half // 8, tile, (zero,) * (3 * point_count))
        spread = jnp.zeros((readers, columns), F32)
        for p in range(point_count):
            around, up, along = acc[3 * p : 3 * p + 3]
            terms = (around * turn_ref[0:1, :], around * turn_ref[1:2, :], up)
            for c in range(3):
                value = jnp.sum(terms[c] + along * xs[p][c], axis=1, keepdims=True)
                spread = jnp.where(kind == c * point_count + p, value, spread)
        spread_scr[rows, :] = jnp.where(lane_slot == slot_ref[rows, :], spread, 0.0)
        return carry

    lax.fori_loop(0, drops, one_drop, 0)
    devices = out_ref.shape[0]
    to = lax.broadcasted_iota(jnp.int32, (devices, entries), 0) == dest_ref[...]
    to = to.astype(F32).astype(BF16)
    spread = spread_scr[...]
    coarse = spread.astype(BF16)
    fine = (spread - coarse.astype(F32)).astype(BF16)
    out_ref[...] = jnp.dot(to, coarse, preferred_element_type=F32) + jnp.dot(
        to, fine, preferred_element_type=F32
    )


def near(index, slot, dest, sep, points, radius, load, tables, normals, devices, columns):
    legendre, fourier, weight, sine, cosine, lon = tables
    drops, degrees, width = radius.shape
    half = degrees // 2
    turn = jnp.asarray(np.stack([np.cos(lon), np.sin(lon)]), F32)
    tilt = np.stack([sine[:half], cosine[:half]])
    tilt = jnp.asarray(np.broadcast_to(tilt[:, :, None], (2, half, width)), F32)
    entries = index.shape[0]
    return pl.pallas_call(
        functools.partial(near_kernel, normals),
        in_specs=[pl.BlockSpec(memory_space=pltpu.VMEM)] * 9,
        out_specs=pl.BlockSpec(memory_space=pltpu.VMEM),
        out_shape=jax.ShapeDtypeStruct((devices, columns), F32),
        scratch_shapes=[pltpu.VMEM((entries, LANES), F32), pltpu.VMEM((entries, columns), F32)],
        compiler_params=pltpu.CompilerParams(vmem_limit_bytes=32 << 20),
        cost_estimate=pl.CostEstimate(
            flops=entries * 4 * 8192 * 20, bytes_accessed=2_000_000, transcendentals=entries * 32768
        ),
    )(index, slot, dest, sep, points, radius, load, turn, tilt)


def per_device(
    coeffs, degree, material, split_coeffs, split_material, separation, reader_dev, reader_slot
):
    drops, fields, degrees, width = coeffs.shape
    readers = reader_dev.shape[1]
    entries = drops * readers
    row_count, col_count = lax.axis_size("row"), lax.axis_size("col")
    devices = row_count * col_count
    tables = spectral_tables(degrees)
    legendre, fourier, weight, sine, cosine, lon = tables
    nlat, nlon = degrees, 2 * degrees

    lat_points = range(nlat // 4, nlat, nlat // 2)
    lon_points = range(0, nlon, nlon // 2)
    spots = [(j, k) for j in lat_points for k in lon_points]
    normals = [
        (
            float(sine[j] * math.cos(lon[k])),
            float(sine[j] * math.sin(lon[k])),
            float(cosine[j]),
        )
        for j, k in spots
    ]
    order = np.arange(width) % degrees
    basis = jnp.asarray(
        np.stack([legendre[order, j, :].T * fourier[:, k][None, :] for j, k in spots]), F32
    )
    keep = (jnp.arange(degrees, dtype=jnp.int32)[None, :] <= degree[:, None]).astype(F32)
    shape = coeffs[:, 0] * keep[:, :, None]
    points = jnp.exp(jnp.sum(shape[:, None] * basis[None], axis=(2, 3))).astype(BF16)
    all_points = lax.all_gather(points, ("row", "col"), axis=0, tiled=True)

    split_count = split_coeffs.shape[0]
    share = split_count // 2
    half_orders = split_coeffs.shape[3] // 2
    row, col = lax.axis_index("row"), lax.axis_index("col")
    parity = row % 2
    route = [(r, r ^ 1) for r in range(row_count)]
    mine = lax.dynamic_slice_in_dim(split_coeffs, parity * share, share, 0)
    theirs = lax.dynamic_slice_in_dim(split_coeffs, (1 - parity) * share, share, 0)
    came = lax.ppermute(theirs.astype(BF16), "row", route).astype(F32)

    traction_coeffs, radius, load = spectral(coeffs, degree, material, tables)

    wide = (share, fields, degrees, 2, half_orders)
    mine, came = mine.reshape(wide), came.reshape(wide)
    lower = jnp.where(parity == 0, mine, came)
    upper = jnp.where(parity == 0, came, mine)
    full = jnp.stack([lower, upper], axis=4).reshape(share, fields, degrees, width)
    pair_start = (row // 2 * col_count + col) * split_count + parity * share
    own_material = lax.dynamic_slice_in_dim(split_material, pair_start, share, 0)
    top = jnp.full((share,), degrees - 1, jnp.int32)
    split_out, _, _ = spectral(full, top, own_material, tables)
    cut = split_out.reshape(share, degrees, 2, 2, half_orders)
    kept = jnp.where(parity == 0, cut[:, :, :, 0], cut[:, :, :, 1])
    given = jnp.where(parity == 0, cut[:, :, :, 1], cut[:, :, :, 0]).astype(BF16)
    kept = kept.reshape(share, degrees, 2 * half_orders)
    got = lax.ppermute(given.reshape(kept.shape), "row", route).astype(F32)

    point_count = len(spots)
    columns = -(-3 * drops * point_count // LANES) * LANES
    table = jnp.pad(all_points, ((0, 0), (0, LANES - point_count)))
    dest = reader_dev.reshape(1, entries)
    index = (reader_dev * drops + reader_slot).reshape(entries, 1)
    slot = reader_slot.reshape(entries, 1)
    sep = jnp.transpose(separation.reshape(3, entries))
    sent = near(
        index, slot, dest, sep, table, radius, load, tables, normals, devices, columns
    )
    received = lax.all_to_all(sent, ("row", "col"), split_axis=0, concat_axis=0, tiled=True)
    velocity = jnp.sum(received, axis=0)[: 3 * drops * point_count]
    split_traction = jnp.where(
        parity == 0, jnp.concatenate([kept, got]), jnp.concatenate([got, kept])
    )
    return traction_coeffs, split_traction, velocity.reshape(3, drops * point_count)


def solution(mesh):
    both = ("row", "col")
    in_specs = (
        P(both, None, None, None),
        P(both),
        P(both, None),
        P(both, None, None, None),
        P(),
        P(None, both, None),
        P(both, None),
        P(both, None),
    )
    out_specs = (P(both, None, None), P(both, None, None), P(None, both))
    return jax.shard_map(
        per_device, mesh=mesh, in_specs=in_specs, out_specs=out_specs, check_vma=False
    )
```

```python
import functools
import math

import jax
import jax.numpy as jnp
import numpy as np
from jax import lax
from jax.experimental import pallas as pl
from jax.experimental.pallas import tpu as pltpu
from jax.sharding import PartitionSpec as P

SOFTENING = 0.04
LANES = 128
F32 = jnp.float32
BF16 = jnp.bfloat16
MESH = pl.DeviceIdType.MESH


def spectral_tables(degrees):
    nlon = 2 * degrees
    theta = (np.arange(degrees) + 0.5) * (math.pi / degrees)
    cosine, sine = np.cos(theta), np.sin(theta)
    legendre = np.zeros((degrees, degrees, degrees))
    for order in range(degrees):
        total = sum(math.log((2.0 * i + 1.0) / (2.0 * i)) for i in range(1, order + 1))
        older = np.exp(0.5 * total + order * np.log(sine)) / math.sqrt(4.0 * math.pi)
        legendre[order, :, order] = older
        if order + 1 < degrees:
            newer = math.sqrt(2.0 * order + 3.0) * cosine * older
            legendre[order, :, order + 1] = newer
            for l in range(order + 2, degrees):
                a = math.sqrt((4.0 * l * l - 1.0) / (l * l - order * order))
                b = math.sqrt(((l - 1.0) ** 2 - order * order) / (4.0 * (l - 1.0) ** 2 - 1.0))
                older, newer = newer, a * (cosine * newer - b * older)
                legendre[order, :, l] = newer
    phase = np.arange(degrees)[:, None] * np.arange(nlon)[None, :] % nlon * (2.0 * math.pi / nlon)
    fourier = np.concatenate([np.cos(phase), np.sin(phase)], axis=0)
    weight = sine * (math.pi / degrees) * (2.0 * math.pi / nlon)
    lon = np.arange(nlon) * (2.0 * math.pi / nlon)
    return legendre, fourier, weight, sine, cosine, lon


def parity_tables(legendre, weight):
    degrees = legendre.shape[0]
    half = degrees // 2
    order = np.arange(2 * degrees) % degrees
    by_lane = legendre[order]
    step = np.arange(half)
    even = np.zeros((half, half, 2 * degrees))
    odd = np.zeros((half, half, 2 * degrees))
    for lane, m in enumerate(order):
        even[:, :, lane] = by_lane[lane][:half, 2 * step + m % 2].T
        odd[:, :, lane] = by_lane[lane][:half, 2 * step + 1 - m % 2].T
    scale = weight[:half, None, None]
    back_even = np.transpose(even, (1, 0, 2)) * scale
    back_odd = np.transpose(odd, (1, 0, 2)) * scale
    return [np.asarray(t, np.float32) for t in (even, odd, back_even, back_odd)]


def spectral_kernel(
    degree_ref, material_ref, coeffs_ref, even_ref, odd_ref, back_even_ref, back_odd_ref,
    fourier_ref, project_ref, weight_ref, out_ref, radius_ref, load_ref,
    field_scr, part_scr, line_scr, back_scr,
):
    count, fields, degrees, width = coeffs_ref.shape
    half = degrees // 2
    first = pl.program_id(0) * count
    level = lax.broadcasted_iota(jnp.int32, (degrees, width), 0)
    levelf = level.astype(F32)
    curve = levelf * (levelf + 1.0) * (1.0 / (degrees * degrees))
    viscous = (levelf + 2.0) * (6.0 / degrees)
    half_level = lax.broadcasted_iota(jnp.int32, (half, width), 0)
    even_order = lax.broadcasted_iota(jnp.int32, (half, width), 1) % 2 == 0

    for d in range(count):
        degree = degree_ref[first + d]
        tension = material_ref[2 * (first + d)]
        viscosity = material_ref[2 * (first + d) + 1]
        keep = level <= degree
        shape = jnp.where(keep, coeffs_ref[d, 0], 0.0)
        field_scr[d, 0] = shape
        field_scr[d, 1] = shape * (tension * curve) + jnp.where(
            keep, coeffs_ref[d, 2] * (viscosity * viscous), 0.0
        )
        field_scr[d, 2] = jnp.where(keep, 3.0 * coeffs_ref[d, 1], 0.0)
        for f in range(3):
            low = field_scr[d, f, pl.ds(0, half, stride=2), :]
            high = field_scr[d, f, pl.ds(1, half, stride=2), :]
            part_scr[d, 2 * f] = jnp.where(even_order, low, high)
            part_scr[d, 2 * f + 1] = jnp.where(even_order, high, low)

    def synth(d, carry):
        total = [jnp.zeros((half, width), F32) for _ in range(6)]
        for i in range(half):
            pe, po = even_ref[i], odd_ref[i]
            for f in range(3):
                total[2 * f] = total[2 * f] + pe * part_scr[d, 2 * f, i : i + 1, :]
                total[2 * f + 1] = total[2 * f + 1] + po * part_scr[d, 2 * f + 1, i : i + 1, :]
        for f in range(3):
            for side in range(2):
                rows = total[2 * f] - total[2 * f + 1] if side else total[2 * f] + total[2 * f + 1]
                coarse = rows.astype(BF16)
                base = pl.multiple_of(((d * 3 + f) * 2 + side) * half, half)
                line_scr[pl.ds(base, half), :width] = coarse
                line_scr[pl.ds(base, half), width:] = (rows - coarse.astype(F32)).astype(BF16)
        return carry

    lax.fori_loop(0, count, synth, 0)
    for d in range(count):
        lines = line_scr[d * 3 * degrees : (d + 1) * 3 * degrees, :]
        surface = jnp.dot(lines, fourier_ref[...], preferred_element_type=F32)
        surface = surface[:, :width] + surface[:, width:]
        radius = jnp.exp(surface[:degrees])
        potential = surface[2 * degrees :]
        traction = surface[degrees : 2 * degrees] + 0.5 * potential * potential
        radius_ref[d] = radius
        load_ref[d] = traction * radius * radius * weight_ref[...]
        project = jnp.dot(traction.astype(BF16), project_ref[...], preferred_element_type=F32)
        back_scr[d, 0] = project[:half] + project[half:]
        back_scr[d, 1] = project[:half] - project[half:]
    pair = math.gcd(count, 2)

    def analyse(block, carry):
        total = [jnp.zeros((half, width), F32) for _ in range(2 * pair)]
        for j in range(half):
            pe, po = back_even_ref[j], back_odd_ref[j]
            for n in range(pair):
                d = block * pair + n
                total[2 * n] = total[2 * n] + pe * back_scr[d, 0, j : j + 1, :]
                total[2 * n + 1] = total[2 * n + 1] + po * back_scr[d, 1, j : j + 1, :]
        for n in range(pair):
            d = block * pair + n
            degree = degree_ref[first + d]
            low, high = total[2 * n], total[2 * n + 1]
            out_ref[d, pl.ds(0, half, stride=2), :] = jnp.where(
                2 * half_level <= degree, jnp.where(even_order, low, high), 0.0
            )
            out_ref[d, pl.ds(1, half, stride=2), :] = jnp.where(
                2 * half_level + 1 <= degree, jnp.where(even_order, high, low), 0.0
            )
        return carry

    lax.fori_loop(0, count // pair, analyse, 0)


def spectral(coeffs, degree, material, tables):
    drops, fields, degrees, width = coeffs.shape
    legendre, fourier, weight, sine, cosine, lon = tables
    half = degrees // 2
    block = math.gcd(drops, 4)
    f32 = jnp.asarray(fourier, F32)
    coarse = f32.astype(BF16)
    fine = (f32 - coarse.astype(F32)).astype(BF16)
    fourier_parts = jnp.concatenate(
        [
            jnp.concatenate([coarse, fine], axis=1),
            jnp.concatenate([coarse, jnp.zeros_like(fine)], axis=1),
        ]
    )
    project = jnp.asarray(fourier.T, BF16)
    folded = np.concatenate([weight[:half], weight[:half]]) / (8.0 * math.pi)
    weight_grid = jnp.asarray(np.broadcast_to(folded[:, None], (degrees, width)), F32)
    parity = [jnp.asarray(t) for t in parity_tables(legendre, weight)]
    whole = lambda a: pl.BlockSpec(a.shape, lambda i: (0,) * a.ndim)
    smem = pl.BlockSpec(memory_space=pltpu.SMEM)
    consts = parity + [fourier_parts, project, weight_grid]
    grid_spec = pl.BlockSpec((block, degrees, width), lambda i: (i, 0, 0))
    return pl.pallas_call(
        spectral_kernel,
        grid=(drops // block,),
        in_specs=[smem, smem, pl.BlockSpec((block, fields, degrees, width), lambda i: (i, 0, 0, 0))]
        + [whole(a) for a in consts],
        out_specs=[grid_spec] * 3,
        out_shape=[jax.ShapeDtypeStruct((drops, degrees, width), F32)] * 3,
        scratch_shapes=[
            pltpu.VMEM((block, 3, degrees, width), F32),
            pltpu.VMEM((block, 6, half, width), F32),
            pltpu.VMEM((block * 3 * degrees, 2 * width), BF16),
            pltpu.VMEM((block, 2, half, width), F32),
        ],
        compiler_params=pltpu.CompilerParams(vmem_limit_bytes=32 << 20),
        cost_estimate=pl.CostEstimate(
            flops=drops * 5_000_000, bytes_accessed=drops * 300_000, transcendentals=drops * 8192
        ),
    )(degree, material.reshape(-1), coeffs, *consts)


def place(index):
    col_count = lax.axis_size("col")
    return (index // col_count, index % col_count)


def own_index():
    return lax.axis_index("row") * lax.axis_size("col") + lax.axis_index("col")


def greet(devices, me):
    barrier = pltpu.get_barrier_semaphore()

    def one(step, carry):
        pl.semaphore_signal(
            barrier, inc=1, device_id=place((me + step) % devices), device_id_type=MESH
        )
        return carry

    lax.fori_loop(1, devices, one, 0)
    return barrier


def points_kernel(
    degree_ref, coeffs_ref, basis_ref, out_ref, shape_scr, part_scr, send_scr, land_scr,
    local_sem, send_sem, recv_sem,
):
    devices = out_ref.shape[0]
    drops, fields, degrees, width = coeffs_ref.shape
    point_count = basis_ref.shape[0]
    me = own_index()
    load = pltpu.make_async_copy(coeffs_ref.at[:, 0], shape_scr, local_sem)
    load.start()
    barrier = greet(devices, me)
    load.wait()
    level = lax.broadcasted_iota(jnp.int32, (degrees, width), 0)
    for d in range(drops):
        shape = jnp.where(level <= degree_ref[d], shape_scr[d], 0.0)
        for p in range(point_count):
            part_scr[p, d : d + 1, :] = jnp.sum(shape * basis_ref[p], axis=0, keepdims=True)
    lane = lax.broadcasted_iota(jnp.int32, (drops, LANES), 1)
    surface = jnp.zeros((drops, LANES), F32)
    for p in range(point_count):
        surface = jnp.where(lane == p, jnp.sum(part_scr[p], axis=1, keepdims=True), surface)
    send_scr[...] = jnp.exp(surface).astype(BF16)
    pl.semaphore_wait(barrier, devices - 1)

    def copy(step):
        return pltpu.make_async_remote_copy(
            src_ref=send_scr,
            dst_ref=land_scr.at[me],
            send_sem=send_sem.at[step],
            recv_sem=recv_sem.at[step],
            device_id=place((me + step) % devices),
            device_id_type=MESH,
        )

    def begin(step, carry):
        copy(step).start()
        return carry

    def finish(step, carry):
        copy(step).wait()
        return carry

    lax.fori_loop(1, devices, begin, 0)
    land_scr[me] = send_scr[...]
    lax.fori_loop(1, devices, finish, 0)
    out_ref[...] = land_scr[...]


def gather_points(degree, coeffs, basis, devices):
    drops, fields, degrees, width = coeffs.shape
    point_count = basis.shape[0]
    vmem = pl.BlockSpec(memory_space=pltpu.VMEM)
    return pl.pallas_call(
        points_kernel,
        in_specs=[
            pl.BlockSpec(memory_space=pltpu.SMEM), pl.BlockSpec(memory_space=pl.ANY), vmem
        ],
        out_specs=vmem,
        out_shape=jax.ShapeDtypeStruct((devices, drops, LANES), BF16),
        scratch_shapes=[
            pltpu.VMEM((drops, degrees, width), F32),
            pltpu.VMEM((point_count, drops, width), F32),
            pltpu.VMEM((drops, LANES), BF16),
            pltpu.VMEM((devices, drops, LANES), BF16),
            pltpu.SemaphoreType.DMA,
            pltpu.SemaphoreType.DMA((devices,)),
            pltpu.SemaphoreType.DMA((devices,)),
        ],
        compiler_params=pltpu.CompilerParams(
            collective_id=0, has_side_effects=True, vmem_limit_bytes=32 << 20
        ),
    )(degree, coeffs, basis)


def near_kernel(
    normals, entry_ref, points_ref, radius_ref, load_ref, turn_ref, tilt_ref, out_ref,
    target_scr, spread_scr, total_scr, send_scr, land_scr, send_sem, recv_sem,
):
    drops, degrees, width = radius_ref.shape
    devices = land_scr.shape[0]
    me = own_index()
    barrier = greet(devices, me)
    entries = entry_ref.shape[0]
    readers = entries // drops
    half = degrees // 2
    targets = points_ref.shape[0]
    columns = spread_scr.shape[1]
    point_count = len(normals)
    to = entry_ref[:, 3:4].astype(jnp.int32)
    slot = entry_ref[:, 4:5].astype(jnp.int32)
    pick = lax.broadcasted_iota(jnp.int32, (entries, targets), 1) == to * drops + slot
    target_scr[...] = jnp.dot(
        pick.astype(F32).astype(BF16), points_ref[...], preferred_element_type=F32
    )
    lane = lax.broadcasted_iota(jnp.int32, (readers, columns), 1)
    block = drops * point_count
    kind = lane // block * point_count + lane % point_count
    lane_slot = lane % block // point_count

    def one_drop(d, carry):
        rows = pl.ds(pl.multiple_of(d * readers, readers), readers)
        sep = entry_ref[rows, :]
        reach = target_scr[rows, :]
        xs, ring, height, square = [], [], [], []
        for p in range(point_count):
            at = reach[:, p : p + 1]
            x = [
                jnp.broadcast_to(sep[:, c : c + 1] + at * normals[p][c], (readers, width))
                for c in range(3)
            ]
            xs.append(x)
            ring.append(x[0] * turn_ref[0:1, :] + x[1] * turn_ref[1:2, :])
            height.append(x[2])
            square.append(x[0] * x[0] + x[1] * x[1] + x[2] * x[2] + SOFTENING)

        def cell(a, r, rr, h, sq):
            off = a - r
            m = r * off
            t = (sq - rr) - m
            rho = t - m
            inv = lax.rsqrt(rho)
            g = (inv * h) * (inv * inv)
            return g * ((rho - m) + SOFTENING), g * off

        def tile(jt, acc):
            acc = list(acc)
            base = pl.multiple_of(jt * 8, 8)
            for q in range(8):
                j = base + q
                r0 = radius_ref[d, pl.ds(j, 1), :]
                r1 = radius_ref[d, pl.ds(j + half, 1), :]
                h0 = load_ref[d, pl.ds(j, 1), :]
                h1 = load_ref[d, pl.ds(j + half, 1), :]
                s = tilt_ref[0, pl.ds(j, 1), :]
                c = tilt_ref[1, pl.ds(j, 1), :]
                q0, q1 = r0 * r0, r1 * r1
                for p in range(point_count):
                    flat = s * ring[p]
                    up = c * height[p]
                    w0, v0 = cell(flat + up, r0, q0, h0, square[p])
                    w1, v1 = cell(flat - up, r1, q1, h1, square[p])
                    acc[3 * p] = acc[3 * p] + s * (w0 + w1)
                    acc[3 * p + 1] = acc[3 * p + 1] + c * (w0 - w1)
                    acc[3 * p + 2] = acc[3 * p + 2] + (v0 + v1)
            return tuple(acc)

        zero = jnp.zeros((readers, width), F32)
        acc = lax.fori_loop(0, half // 8, tile, (zero,) * (3 * point_count))
        spread = jnp.zeros((readers, columns), F32)
        for p in range(point_count):
            around, up, along = acc[3 * p : 3 * p + 3]
            terms = (around * turn_ref[0:1, :], around * turn_ref[1:2, :], up)
            for c in range(3):
                value = jnp.sum(terms[c] + along * xs[p][c], axis=1, keepdims=True)
                spread = jnp.where(kind == c * point_count + p, value, spread)
        spread_scr[rows, :] = jnp.where(
            lane_slot == sep[:, 4:5].astype(jnp.int32), spread, 0.0
        )
        return carry

    lax.fori_loop(0, drops, one_drop, 0)
    goes = lax.broadcasted_iota(jnp.int32, (entries, devices), 1) == to
    goes = goes.astype(F32).astype(BF16)
    spread = spread_scr[...]
    coarse = spread.astype(BF16)
    fine = (spread - coarse.astype(F32)).astype(BF16)
    first = (((0,), (0,)), ((), ()))
    total_scr[...] = lax.dot_general(
        goes, coarse, first, preferred_element_type=F32
    ) + lax.dot_general(goes, fine, first, preferred_element_type=F32)

    def lay(device, carry):
        send_scr[device] = total_scr[pl.ds(device, 1), :]
        return carry

    lax.fori_loop(0, devices, lay, 0)
    pl.semaphore_wait(barrier, devices - 1)

    def copy(step):
        other = (me + step) % devices
        return pltpu.make_async_remote_copy(
            src_ref=send_scr.at[other],
            dst_ref=land_scr.at[me],
            send_sem=send_sem.at[step],
            recv_sem=recv_sem.at[step],
            device_id=place(other),
            device_id_type=MESH,
        )

    def begin(step, carry):
        copy(step).start()
        return carry

    def finish(step, carry):
        copy(step).wait()
        return carry

    lax.fori_loop(1, devices, begin, 0)
    land_scr[me] = send_scr[me]
    lax.fori_loop(1, devices, finish, 0)
    velocity = jnp.sum(land_scr[...], axis=0)
    for c in range(3):
        out_ref[c : c + 1, :] = velocity[:, c * block : (c + 1) * block]


def near(entry, points, radius, load, tables, normals, devices, columns):
    legendre, fourier, weight, sine, cosine, lon = tables
    drops, degrees, width = radius.shape
    half = degrees // 2
    turn = jnp.asarray(np.stack([np.cos(lon), np.sin(lon)]), F32)
    tilt = np.stack([sine[:half], cosine[:half]])
    tilt = jnp.asarray(np.broadcast_to(tilt[:, :, None], (2, half, width)), F32)
    entries = entry.shape[0]
    return pl.pallas_call(
        functools.partial(near_kernel, normals),
        in_specs=[pl.BlockSpec(memory_space=pltpu.VMEM)] * 6,
        out_specs=pl.BlockSpec(memory_space=pltpu.VMEM),
        out_shape=jax.ShapeDtypeStruct((3, drops * len(normals)), F32),
        scratch_shapes=[
            pltpu.VMEM((entries, LANES), F32),
            pltpu.VMEM((entries, columns), F32),
            pltpu.VMEM((devices, columns), F32),
            pltpu.VMEM((devices, 1, columns), F32),
            pltpu.VMEM((devices, 1, columns), F32),
            pltpu.SemaphoreType.DMA((devices,)),
            pltpu.SemaphoreType.DMA((devices,)),
        ],
        compiler_params=pltpu.CompilerParams(
            collective_id=1, has_side_effects=True, vmem_limit_bytes=32 << 20
        ),
        cost_estimate=pl.CostEstimate(
            flops=entries * 4 * 8192 * 20, bytes_accessed=2_000_000, transcendentals=entries * 32768
        ),
    )(entry, points, radius, load, turn, tilt)


def per_device(
    coeffs, degree, material, split_coeffs, split_material, separation, reader_dev, reader_slot
):
    drops, fields, degrees, width = coeffs.shape
    readers = reader_dev.shape[1]
    entries = drops * readers
    row_count, col_count = lax.axis_size("row"), lax.axis_size("col")
    devices = row_count * col_count
    tables = spectral_tables(degrees)
    legendre, fourier, weight, sine, cosine, lon = tables
    nlat, nlon = degrees, 2 * degrees

    lat_points = range(nlat // 4, nlat, nlat // 2)
    lon_points = range(0, nlon, nlon // 2)
    spots = [(j, k) for j in lat_points for k in lon_points]
    normals = [
        (
            float(sine[j] * math.cos(lon[k])),
            float(sine[j] * math.sin(lon[k])),
            float(cosine[j]),
        )
        for j, k in spots
    ]
    order = np.arange(width) % degrees
    basis = jnp.asarray(
        np.stack([legendre[order, j, :].T * fourier[:, k][None, :] for j, k in spots]), F32
    )
    all_points = gather_points(degree, coeffs, basis, devices)

    split_count = split_coeffs.shape[0]
    share = split_count // 2
    half_orders = split_coeffs.shape[3] // 2
    row, col = lax.axis_index("row"), lax.axis_index("col")
    parity = row % 2
    route = [(r, r ^ 1) for r in range(row_count)]
    mine = lax.dynamic_slice_in_dim(split_coeffs, parity * share, share, 0)
    theirs = lax.dynamic_slice_in_dim(split_coeffs, (1 - parity) * share, share, 0)
    came = lax.ppermute(theirs.astype(BF16), "row", route).astype(F32)

    traction_coeffs, radius, load = spectral(coeffs, degree, material, tables)

    wide = (share, fields, degrees, 2, half_orders)
    mine, came = mine.reshape(wide), came.reshape(wide)
    lower = jnp.where(parity == 0, mine, came)
    upper = jnp.where(parity == 0, came, mine)
    full = jnp.stack([lower, upper], axis=4).reshape(share, fields, degrees, width)
    pair_start = (row // 2 * col_count + col) * split_count + parity * share
    own_material = lax.dynamic_slice_in_dim(split_material, pair_start, share, 0)
    top = jnp.full((share,), degrees - 1, jnp.int32)
    split_out, _, _ = spectral(full, top, own_material, tables)
    cut = split_out.reshape(share, degrees, 2, 2, half_orders)
    kept = jnp.where(parity == 0, cut[:, :, :, 0], cut[:, :, :, 1])
    given = jnp.where(parity == 0, cut[:, :, :, 1], cut[:, :, :, 0]).astype(BF16)
    kept = kept.reshape(share, degrees, 2 * half_orders)
    got = lax.ppermute(given.reshape(kept.shape), "row", route).astype(F32)

    point_count = len(spots)
    columns = -(-3 * drops * point_count // LANES) * LANES
    entry = jnp.concatenate(
        [
            jnp.transpose(separation, (1, 2, 0)),
            reader_dev.astype(F32)[:, :, None],
            reader_slot.astype(F32)[:, :, None],
        ],
        axis=2,
    ).reshape(entries, 5)
    table = all_points.reshape(devices * drops, LANES)
    velocity = near(entry, table, radius, load, tables, normals, devices, columns)
    split_traction = jnp.where(
        parity == 0, jnp.concatenate([kept, got]), jnp.concatenate([got, kept])
    )
    return traction_coeffs, split_traction, velocity


def solution(mesh):
    both = ("row", "col")
    in_specs = (
        P(both, None, None, None),
        P(both),
        P(both, None),
        P(both, None, None, None),
        P(),
        P(None, both, None),
        P(both, None),
        P(both, None),
    )
    out_specs = (P(both, None, None), P(both, None, None), P(None, both))
    return jax.shard_map(
        per_device, mesh=mesh, in_specs=in_specs, out_specs=out_specs, check_vma=False
    )
```

```python
import functools
import math

import jax
import jax.numpy as jnp
import numpy as np
from jax import lax
from jax.experimental import pallas as pl
from jax.experimental.pallas import tpu as pltpu
from jax.sharding import PartitionSpec as P

SOFTENING = 0.04
LANES = 128
F32 = jnp.float32
BF16 = jnp.bfloat16
MESH = pl.DeviceIdType.MESH


def spectral_tables(degrees):
    nlon = 2 * degrees
    theta = (np.arange(degrees) + 0.5) * (math.pi / degrees)
    cosine, sine = np.cos(theta), np.sin(theta)
    legendre = np.zeros((degrees, degrees, degrees))
    for order in range(degrees):
        total = sum(math.log((2.0 * i + 1.0) / (2.0 * i)) for i in range(1, order + 1))
        older = np.exp(0.5 * total + order * np.log(sine)) / math.sqrt(4.0 * math.pi)
        legendre[order, :, order] = older
        if order + 1 < degrees:
            newer = math.sqrt(2.0 * order + 3.0) * cosine * older
            legendre[order, :, order + 1] = newer
            for l in range(order + 2, degrees):
                a = math.sqrt((4.0 * l * l - 1.0) / (l * l - order * order))
                b = math.sqrt(((l - 1.0) ** 2 - order * order) / (4.0 * (l - 1.0) ** 2 - 1.0))
                older, newer = newer, a * (cosine * newer - b * older)
                legendre[order, :, l] = newer
    phase = np.arange(degrees)[:, None] * np.arange(nlon)[None, :] % nlon * (2.0 * math.pi / nlon)
    fourier = np.concatenate([np.cos(phase), np.sin(phase)], axis=0)
    weight = sine * (math.pi / degrees) * (2.0 * math.pi / nlon)
    lon = np.arange(nlon) * (2.0 * math.pi / nlon)
    return legendre, fourier, weight, sine, cosine, lon


def parity_tables(legendre, weight):
    degrees = legendre.shape[0]
    half = degrees // 2
    order = np.arange(2 * degrees) % degrees
    by_lane = legendre[order]
    step = np.arange(half)
    even = np.zeros((half, half, 2 * degrees))
    odd = np.zeros((half, half, 2 * degrees))
    for lane, m in enumerate(order):
        even[:, :, lane] = by_lane[lane][:half, 2 * step + m % 2].T
        odd[:, :, lane] = by_lane[lane][:half, 2 * step + 1 - m % 2].T
    scale = weight[:half, None, None]
    back_even = np.transpose(even, (1, 0, 2)) * scale
    back_odd = np.transpose(odd, (1, 0, 2)) * scale
    return [np.asarray(t, np.float32) for t in (even, odd, back_even, back_odd)]


def peers():
    rows, cols = lax.axis_size("row"), lax.axis_size("col")
    row, col = lax.axis_index("row"), lax.axis_index("col")
    result = []
    for step in range(1, rows * cols):
        r, c = row + step // cols, col + step % cols
        result.append((jnp.where(r >= rows, r - rows, r), jnp.where(c >= cols, c - cols, c)))
    return result


def own_index():
    return lax.axis_index("row") * lax.axis_size("col") + lax.axis_index("col")


def greet():
    barrier = pltpu.get_barrier_semaphore()
    for peer in peers():
        pl.semaphore_signal(barrier, inc=1, device_id=peer, device_id_type=MESH)
    return barrier


def to_all(source, land, send_sem, recv_sem):
    copies = []
    for n, peer in enumerate(peers()):
        copies.append(
            pltpu.make_async_remote_copy(
                src_ref=source(peer),
                dst_ref=land.at[own_index()],
                send_sem=send_sem.at[n],
                recv_sem=recv_sem.at[n],
                device_id=peer,
                device_id_type=MESH,
            )
        )
    return copies


def to_partner(source, land, send_sem, recv_sem):
    row = lax.axis_index("row")
    return pltpu.make_async_remote_copy(
        src_ref=source,
        dst_ref=land,
        send_sem=send_sem,
        recv_sem=recv_sem,
        device_id=(row + 1 - 2 * (row % 2), lax.axis_index("col")),
        device_id_type=MESH,
    )


def spectral_body(coeffs_ref, scalars, consts, out_ref, radius_ref, load_ref, scratch):
    even_ref, odd_ref, back_even_ref, back_odd_ref, fourier_ref, project_ref, weight_ref = consts
    field_scr, part_scr, line_scr, back_scr = scratch
    count, fields, degrees, width = coeffs_ref.shape
    half = degrees // 2
    level = lax.broadcasted_iota(jnp.int32, (degrees, width), 0)
    levelf = level.astype(F32)
    curve = levelf * (levelf + 1.0) * (1.0 / (degrees * degrees))
    viscous = (levelf + 2.0) * (6.0 / degrees)
    half_level = lax.broadcasted_iota(jnp.int32, (half, width), 0)
    even_order = lax.broadcasted_iota(jnp.int32, (half, width), 1) % 2 == 0

    for d in range(count):
        degree, tension, viscosity = scalars(d)
        keep = level <= degree
        shape = jnp.where(keep, coeffs_ref[d, 0], 0.0)
        field_scr[d, 0] = shape
        field_scr[d, 1] = shape * (tension * curve) + jnp.where(
            keep, coeffs_ref[d, 2] * (viscosity * viscous), 0.0
        )
        field_scr[d, 2] = jnp.where(keep, 3.0 * coeffs_ref[d, 1], 0.0)
        for f in range(3):
            low = field_scr[d, f, pl.ds(0, half, stride=2), :]
            high = field_scr[d, f, pl.ds(1, half, stride=2), :]
            part_scr[d, 2 * f] = jnp.where(even_order, low, high)
            part_scr[d, 2 * f + 1] = jnp.where(even_order, high, low)

    def synth(d, carry):
        total = [jnp.zeros((half, width), F32) for _ in range(6)]
        for i in range(half):
            pe, po = even_ref[i], odd_ref[i]
            for f in range(3):
                total[2 * f] = total[2 * f] + pe * part_scr[d, 2 * f, i : i + 1, :]
                total[2 * f + 1] = total[2 * f + 1] + po * part_scr[d, 2 * f + 1, i : i + 1, :]
        for f in range(3):
            for side in range(2):
                rows = total[2 * f] - total[2 * f + 1] if side else total[2 * f] + total[2 * f + 1]
                coarse = rows.astype(BF16)
                base = pl.multiple_of(((d * 3 + f) * 2 + side) * half, half)
                line_scr[pl.ds(base, half), :width] = coarse
                line_scr[pl.ds(base, half), width:] = (rows - coarse.astype(F32)).astype(BF16)
        return carry

    lax.fori_loop(0, count, synth, 0)
    for d in range(count):
        lines = line_scr[d * 3 * degrees : (d + 1) * 3 * degrees, :]
        surface = jnp.dot(lines, fourier_ref[...], preferred_element_type=F32)
        surface = surface[:, :width] + surface[:, width:]
        potential = surface[2 * degrees :]
        traction = surface[degrees : 2 * degrees] + 0.5 * potential * potential
        if radius_ref is not None:
            radius = jnp.exp(surface[:degrees])
            radius_ref[d] = radius
            load_ref[d] = traction * radius * radius * weight_ref[...]
        project = jnp.dot(traction.astype(BF16), project_ref[...], preferred_element_type=F32)
        back_scr[d, 0] = project[:half] + project[half:]
        back_scr[d, 1] = project[:half] - project[half:]
    pair = math.gcd(count, 2)

    def analyse(block, carry):
        total = [jnp.zeros((half, width), F32) for _ in range(2 * pair)]
        for j in range(half):
            pe, po = back_even_ref[j], back_odd_ref[j]
            for n in range(pair):
                d = block * pair + n
                total[2 * n] = total[2 * n] + pe * back_scr[d, 0, j : j + 1, :]
                total[2 * n + 1] = total[2 * n + 1] + po * back_scr[d, 1, j : j + 1, :]
        for n in range(pair):
            d = block * pair + n
            degree = scalars(d)[0]
            low, high = total[2 * n], total[2 * n + 1]
            out_ref[d, pl.ds(0, half, stride=2), :] = jnp.where(
                2 * half_level <= degree, jnp.where(even_order, low, high), 0.0
            )
            out_ref[d, pl.ds(1, half, stride=2), :] = jnp.where(
                2 * half_level + 1 <= degree, jnp.where(even_order, high, low), 0.0
            )
        return carry

    lax.fori_loop(0, count // pair, analyse, 0)


def spectral_kernel(
    degree_ref, material_ref, split_material_ref, coeffs_ref, all_coeffs_ref, split_ref, basis_ref,
    *rest,
):
    consts, rest = rest[:7], rest[7:]
    out_ref, radius_ref, load_ref, split_out_ref, points_ref = rest[:5]
    scratch, rest = rest[5:9], rest[9:]
    (shape_scr, point_scr, send_scr, land_scr, give_scr, came_scr, full_scr,
     local_sem, send_sem, recv_sem, give_sem, came_sem) = rest
    count, fields, degrees, width = coeffs_ref.shape
    drops = shape_scr.shape[0]
    split_count, half_width = split_ref.shape[0], split_ref.shape[3]
    share, orders = split_count // 2, half_width // 2
    devices = land_scr.shape[0]
    steps = drops // count
    step = pl.program_id(0)
    row, col = lax.axis_index("row"), lax.axis_index("col")
    parity = row % 2
    local = pltpu.make_async_copy(all_coeffs_ref.at[:, 0], shape_scr, local_sem)
    swap = to_partner(give_scr, came_scr, give_sem, came_sem)

    @pl.when(step == 0)
    def _():
        local.start()
        greet()
        give_scr[...] = split_ref[pl.ds((1 - parity) * share, share)].astype(BF16)

    @pl.when(step < steps)
    def _():
        first = step * count

        def scalars(d):
            at = first + d
            return degree_ref[at], material_ref[0, at], material_ref[1, at]

        spectral_body(coeffs_ref, scalars, consts, out_ref, radius_ref, load_ref, scratch)

    @pl.when(step == 0)
    def _():
        local.wait()
        level = lax.broadcasted_iota(jnp.int32, (degrees, width), 0)
        point_count = basis_ref.shape[0]
        for d in range(drops):
            shape = jnp.where(level <= degree_ref[d], shape_scr[d], 0.0)
            for p in range(point_count):
                point_scr[p, d : d + 1, :] = jnp.sum(shape * basis_ref[p], axis=0, keepdims=True)
        lane = lax.broadcasted_iota(jnp.int32, (drops, LANES), 1)
        surface = jnp.zeros((drops, LANES), F32)
        for p in range(point_count):
            surface = jnp.where(lane == p, jnp.sum(point_scr[p], axis=1, keepdims=True), surface)
        send_scr[...] = jnp.exp(surface).astype(BF16)
        pl.semaphore_wait(pltpu.get_barrier_semaphore(), devices - 1)
        swap.start()
        for copy in to_all(lambda peer: send_scr, land_scr, send_sem, recv_sem):
            copy.start()
        land_scr[own_index()] = send_scr[...]

    @pl.when(step == steps)
    def _():
        swap.wait()
        mine = split_ref[pl.ds(parity * share, share)]
        came = came_scr[...].astype(F32)
        for d in range(share):
            for f in range(fields):
                lower = jnp.where(parity == 0, mine[d, f], came[d, f])
                upper = jnp.where(parity == 0, came[d, f], mine[d, f])
                full_scr[d, f] = jnp.concatenate(
                    [lower[:, :orders], upper[:, :orders], lower[:, orders:], upper[:, orders:]],
                    axis=1,
                )
        start = (row // 2 * lax.axis_size("col") + col) * split_count + parity * share

        def scalars(d):
            at = start + d
            return degrees - 1, split_material_ref[0, at], split_material_ref[1, at]

        spectral_body(full_scr, scalars, consts, split_out_ref, None, None, scratch)
        for copy in to_all(lambda peer: send_scr, land_scr, send_sem, recv_sem):
            copy.wait()
        points_ref[...] = land_scr[...]


def spectral(coeffs, degree, material, split_coeffs, split_material, basis, tables, devices):
    drops, fields, degrees, width = coeffs.shape
    split_count, half_width = split_coeffs.shape[0], split_coeffs.shape[3]
    share = split_count // 2
    legendre, fourier, weight, sine, cosine, lon = tables
    half = degrees // 2
    block = math.gcd(drops, 4)
    steps = drops // block
    f32 = jnp.asarray(fourier, F32)
    coarse = f32.astype(BF16)
    fine = (f32 - coarse.astype(F32)).astype(BF16)
    fourier_parts = jnp.concatenate(
        [
            jnp.concatenate([coarse, fine], axis=1),
            jnp.concatenate([coarse, jnp.zeros_like(fine)], axis=1),
        ]
    )
    project = jnp.asarray(fourier.T, BF16)
    folded = np.concatenate([weight[:half], weight[:half]]) / (8.0 * math.pi)
    weight_grid = jnp.asarray(np.broadcast_to(folded[:, None], (degrees, width)), F32)
    parity = [jnp.asarray(t) for t in parity_tables(legendre, weight)]
    smem = pl.BlockSpec(memory_space=pltpu.SMEM)
    vmem = pl.BlockSpec(memory_space=pltpu.VMEM)
    consts = parity + [fourier_parts, project, weight_grid]
    at = lambda i: jnp.minimum(i, steps - 1)
    grid_spec = pl.BlockSpec((block, degrees, width), lambda i: (at(i), 0, 0))
    grid_shape = jax.ShapeDtypeStruct((drops, degrees, width), F32)
    held = (share, fields, degrees, half_width)
    return pl.pallas_call(
        spectral_kernel,
        grid=(steps + 1,),
        in_specs=[
            smem, smem, smem,
            pl.BlockSpec((block, fields, degrees, width), lambda i: (at(i), 0, 0, 0)),
            pl.BlockSpec(memory_space=pl.ANY), vmem, vmem,
        ]
        + [vmem] * len(consts),
        out_specs=[grid_spec] * 3 + [vmem, vmem],
        out_shape=[grid_shape] * 3
        + [
            jax.ShapeDtypeStruct((share, degrees, width), F32),
            jax.ShapeDtypeStruct((devices, drops, LANES), BF16),
        ],
        scratch_shapes=[
            pltpu.VMEM((block, 3, degrees, width), F32),
            pltpu.VMEM((block, 6, half, width), F32),
            pltpu.VMEM((block * 3 * degrees, 2 * width), BF16),
            pltpu.VMEM((block, 2, half, width), F32),
            pltpu.VMEM((drops, degrees, width), F32),
            pltpu.VMEM((basis.shape[0], drops, width), F32),
            pltpu.VMEM((drops, LANES), BF16),
            pltpu.VMEM((devices, drops, LANES), BF16),
            pltpu.VMEM(held, BF16),
            pltpu.VMEM(held, BF16),
            pltpu.VMEM((share, fields, degrees, width), F32),
            pltpu.SemaphoreType.DMA,
            pltpu.SemaphoreType.DMA((devices,)),
            pltpu.SemaphoreType.DMA((devices,)),
            pltpu.SemaphoreType.DMA,
            pltpu.SemaphoreType.DMA,
        ],
        compiler_params=pltpu.CompilerParams(
            collective_id=0, has_side_effects=True, vmem_limit_bytes=40 << 20
        ),
    )(
        degree, material.T, split_material.T, coeffs, coeffs, split_coeffs, basis, *consts
    )


def near_kernel(
    normals, dev_ref, slot_ref, sep_ref, points_ref, radius_ref, load_ref, split_ref,
    turn_ref, tilt_ref, out_ref, split_out_ref,
    entry_ref, target_scr, spread_scr, total_scr, send_scr, land_scr, give_scr, came_scr,
    send_sem, recv_sem, give_sem, came_sem,
):
    drops, degrees, width = radius_ref.shape
    devices = land_scr.shape[0]
    me = own_index()
    barrier = greet()
    readers = dev_ref.shape[0]
    entries = drops * readers
    entry_lane = lax.broadcasted_iota(jnp.int32, (readers, LANES), 1)
    for d in range(drops):
        columns_of = [sep_ref[c, :, d : d + 1] for c in range(3)]
        columns_of += [ref[:, d : d + 1].astype(F32) for ref in (dev_ref, slot_ref)]
        rows_of = jnp.zeros((readers, LANES), F32)
        for n, column in enumerate(columns_of):
            rows_of = jnp.where(entry_lane == n, column, rows_of)
        entry_ref[d * readers : (d + 1) * readers, :] = rows_of
    share, split_width = split_ref.shape[0], split_ref.shape[2]
    orders = split_width // 4
    parity = lax.axis_index("row") % 2
    for n in range(share):
        whole = split_ref[n]
        cut = [whole[:, k * orders : (k + 1) * orders] for k in range(4)]
        lower = jnp.concatenate([cut[0], cut[2]], axis=1)
        upper = jnp.concatenate([cut[1], cut[3]], axis=1)
        give_scr[n] = jnp.where(parity == 0, upper, lower).astype(BF16)
        split_out_ref[parity * share + n] = jnp.where(parity == 0, lower, upper)
    swap = to_partner(give_scr, came_scr, give_sem, came_sem)
    half = degrees // 2
    targets = points_ref.shape[0]
    columns = spread_scr.shape[1]
    point_count = len(normals)
    to = entry_ref[:, 3:4].astype(jnp.int32)
    slot = entry_ref[:, 4:5].astype(jnp.int32)
    pick = lax.broadcasted_iota(jnp.int32, (entries, targets), 1) == to * drops + slot
    target_scr[...] = jnp.dot(
        pick.astype(F32).astype(BF16), points_ref[...], preferred_element_type=F32
    )
    lane = lax.broadcasted_iota(jnp.int32, (readers, columns), 1)
    block = drops * point_count
    kind = lane // block * point_count + lane % point_count
    lane_slot = lane % block // point_count

    def one_drop(d, carry):
        rows = pl.ds(pl.multiple_of(d * readers, readers), readers)
        sep = entry_ref[rows, :]
        reach = target_scr[rows, :]
        xs, ring, height, square = [], [], [], []
        for p in range(point_count):
            at = reach[:, p : p + 1]
            x = [
                jnp.broadcast_to(sep[:, c : c + 1] + at * normals[p][c], (readers, width))
                for c in range(3)
            ]
            xs.append(x)
            ring.append(x[0] * turn_ref[0:1, :] + x[1] * turn_ref[1:2, :])
            height.append(x[2])
            square.append(x[0] * x[0] + x[1] * x[1] + x[2] * x[2] + SOFTENING)

        def cell(a, r, rr, h, sq):
            off = a - r
            m = r * off
            t = (sq - rr) - m
            rho = t - m
            inv = lax.rsqrt(rho)
            g = (inv * h) * (inv * inv)
            return g * ((rho - m) + SOFTENING), g * off

        def tile(jt, acc):
            acc = list(acc)
            base = pl.multiple_of(jt * 8, 8)
            for q in range(8):
                j = base + q
                r0 = radius_ref[d, pl.ds(j, 1), :]
                r1 = radius_ref[d, pl.ds(j + half, 1), :]
                h0 = load_ref[d, pl.ds(j, 1), :]
                h1 = load_ref[d, pl.ds(j + half, 1), :]
                s = tilt_ref[0, pl.ds(j, 1), :]
                c = tilt_ref[1, pl.ds(j, 1), :]
                q0, q1 = r0 * r0, r1 * r1
                for p in range(point_count):
                    flat = s * ring[p]
                    up = c * height[p]
                    w0, v0 = cell(flat + up, r0, q0, h0, square[p])
                    w1, v1 = cell(flat - up, r1, q1, h1, square[p])
                    acc[3 * p] = acc[3 * p] + s * (w0 + w1)
                    acc[3 * p + 1] = acc[3 * p + 1] + c * (w0 - w1)
                    acc[3 * p + 2] = acc[3 * p + 2] + (v0 + v1)
            return tuple(acc)

        zero = jnp.zeros((readers, width), F32)
        acc = lax.fori_loop(0, half // 8, tile, (zero,) * (3 * point_count))
        spread = jnp.zeros((readers, columns), F32)
        for p in range(point_count):
            around, up, along = acc[3 * p : 3 * p + 3]
            terms = (around * turn_ref[0:1, :], around * turn_ref[1:2, :], up)
            for c in range(3):
                value = jnp.sum(terms[c] + along * xs[p][c], axis=1, keepdims=True)
                spread = jnp.where(kind == c * point_count + p, value, spread)
        spread_scr[rows, :] = jnp.where(
            lane_slot == sep[:, 4:5].astype(jnp.int32), spread, 0.0
        )
        return carry

    lax.fori_loop(0, drops // 2, one_drop, 0)
    pl.semaphore_wait(barrier, devices - 1)
    swap.start()
    lax.fori_loop(drops // 2, drops, one_drop, 0)
    goes = lax.broadcasted_iota(jnp.int32, (entries, devices), 1) == to
    goes = goes.astype(F32).astype(BF16)
    spread = spread_scr[...]
    coarse = spread.astype(BF16)
    fine = (spread - coarse.astype(F32)).astype(BF16)
    first = (((0,), (0,)), ((), ()))
    total_scr[...] = lax.dot_general(
        goes, coarse, first, preferred_element_type=F32
    ) + lax.dot_general(goes, fine, first, preferred_element_type=F32)

    for device in range(devices):
        send_scr[device] = total_scr[device : device + 1, :]
    col_count = lax.axis_size("col")
    copies = to_all(
        lambda peer: send_scr.at[peer[0] * col_count + peer[1]], land_scr, send_sem, recv_sem
    )
    for copy in copies:
        copy.start()
    land_scr[me] = send_scr[me]
    swap.wait()
    split_out_ref[pl.ds((1 - parity) * share, share)] = came_scr[...].astype(F32)
    for copy in copies:
        copy.wait()
    velocity = jnp.sum(land_scr[...], axis=0)
    for c in range(3):
        out_ref[c : c + 1, :] = velocity[:, c * block : (c + 1) * block]


def near(dev, slot, sep, points, radius, load, split_out, tables, normals, devices, columns):
    legendre, fourier, weight, sine, cosine, lon = tables
    drops, degrees, width = radius.shape
    share = split_out.shape[0]
    half = degrees // 2
    turn = jnp.asarray(np.stack([np.cos(lon), np.sin(lon)]), F32)
    tilt = np.stack([sine[:half], cosine[:half]])
    tilt = jnp.asarray(np.broadcast_to(tilt[:, :, None], (2, half, width)), F32)
    entries = drops * dev.shape[0]
    vmem = pl.BlockSpec(memory_space=pltpu.VMEM)
    held = (share, degrees, width // 2)
    return pl.pallas_call(
        functools.partial(near_kernel, normals),
        in_specs=[vmem] * 9,
        out_specs=[vmem, vmem],
        out_shape=[
            jax.ShapeDtypeStruct((3, drops * len(normals)), F32),
            jax.ShapeDtypeStruct((2 * share, degrees, width // 2), F32),
        ],
        scratch_shapes=[
            pltpu.VMEM((entries, LANES), F32),
            pltpu.VMEM((entries, LANES), F32),
            pltpu.VMEM((entries, columns), F32),
            pltpu.VMEM((devices, columns), F32),
            pltpu.VMEM((devices, 1, columns), F32),
            pltpu.VMEM((devices, 1, columns), F32),
            pltpu.VMEM(held, BF16),
            pltpu.VMEM(held, BF16),
            pltpu.SemaphoreType.DMA((devices,)),
            pltpu.SemaphoreType.DMA((devices,)),
            pltpu.SemaphoreType.DMA,
            pltpu.SemaphoreType.DMA,
        ],
        compiler_params=pltpu.CompilerParams(
            collective_id=1, has_side_effects=True, vmem_limit_bytes=32 << 20
        ),
        cost_estimate=pl.CostEstimate(
            flops=entries * 4 * 8192 * 20, bytes_accessed=2_000_000, transcendentals=entries * 32768
        ),
    )(dev, slot, sep, points, radius, load, split_out, turn, tilt)


def per_device(
    coeffs, degree, material, split_coeffs, split_material, separation, reader_dev, reader_slot
):
    drops, fields, degrees, width = coeffs.shape
    row_count, col_count = lax.axis_size("row"), lax.axis_size("col")
    devices = row_count * col_count
    tables = spectral_tables(degrees)
    legendre, fourier, weight, sine, cosine, lon = tables
    nlat, nlon = degrees, 2 * degrees

    lat_points = range(nlat // 4, nlat, nlat // 2)
    lon_points = range(0, nlon, nlon // 2)
    spots = [(j, k) for j in lat_points for k in lon_points]
    normals = [
        (
            float(sine[j] * math.cos(lon[k])),
            float(sine[j] * math.sin(lon[k])),
            float(cosine[j]),
        )
        for j, k in spots
    ]
    order = np.arange(width) % degrees
    basis = jnp.asarray(
        np.stack([legendre[order, j, :].T * fourier[:, k][None, :] for j, k in spots]), F32
    )
    traction_coeffs, radius, load, split_out, points = spectral(
        coeffs, degree, material, split_coeffs, split_material, basis, tables, devices
    )
    point_count = len(spots)
    columns = -(-3 * drops * point_count // LANES) * LANES
    velocity, split_traction = near(
        reader_dev.T, reader_slot.T, jnp.transpose(separation, (0, 2, 1)),
        points.reshape(devices * drops, LANES), radius, load, split_out,
        tables, normals, devices, columns,
    )
    return traction_coeffs, split_traction, velocity


def solution(mesh):
    both = ("row", "col")
    in_specs = (
        P(both, None, None, None),
        P(both),
        P(both, None),
        P(both, None, None, None),
        P(),
        P(None, both, None),
        P(both, None),
        P(both, None),
    )
    out_specs = (P(both, None, None), P(both, None, None), P(None, both))
    return jax.shard_map(
        per_device, mesh=mesh, in_specs=in_specs, out_specs=out_specs, check_vma=False
    )
```

```python
import functools
import math

import jax
import jax.numpy as jnp
import ml_dtypes
import numpy as np
from jax import lax
from jax.experimental import pallas as pl
from jax.experimental.pallas import tpu as pltpu
from jax.sharding import PartitionSpec as P

SOFTENING = 0.04
VMEM_BYTES = 60 << 20
LANES = 128
F32 = jnp.float32
BF16 = jnp.bfloat16
MESH = pl.DeviceIdType.MESH


def spectral_tables(degrees):
    nlon = 2 * degrees
    theta = (np.arange(degrees) + 0.5) * (math.pi / degrees)
    cosine, sine = np.cos(theta), np.sin(theta)
    legendre = np.zeros((degrees, degrees, degrees))
    for order in range(degrees):
        total = sum(math.log((2.0 * i + 1.0) / (2.0 * i)) for i in range(1, order + 1))
        older = np.exp(0.5 * total + order * np.log(sine)) / math.sqrt(4.0 * math.pi)
        legendre[order, :, order] = older
        if order + 1 < degrees:
            newer = math.sqrt(2.0 * order + 3.0) * cosine * older
            legendre[order, :, order + 1] = newer
            for l in range(order + 2, degrees):
                a = math.sqrt((4.0 * l * l - 1.0) / (l * l - order * order))
                b = math.sqrt(((l - 1.0) ** 2 - order * order) / (4.0 * (l - 1.0) ** 2 - 1.0))
                older, newer = newer, a * (cosine * newer - b * older)
                legendre[order, :, l] = newer
    phase = np.arange(degrees)[:, None] * np.arange(nlon)[None, :] % nlon * (2.0 * math.pi / nlon)
    fourier = np.concatenate([np.cos(phase), np.sin(phase)], axis=0)
    weight = sine * (math.pi / degrees) * (2.0 * math.pi / nlon)
    lon = np.arange(nlon) * (2.0 * math.pi / nlon)
    return legendre, fourier, weight, sine, cosine, lon


def parity_tables(legendre, weight):
    degrees = legendre.shape[0]
    half = degrees // 2
    order = np.arange(2 * degrees) % degrees
    by_lane = legendre[order]
    step = np.arange(half)
    even = np.zeros((half, half, 2 * degrees))
    odd = np.zeros((half, half, 2 * degrees))
    for lane, m in enumerate(order):
        even[:, :, lane] = by_lane[lane][:half, 2 * step + m % 2].T
        odd[:, :, lane] = by_lane[lane][:half, 2 * step + 1 - m % 2].T
    scale = weight[:half, None, None]
    back_even = np.transpose(even, (1, 0, 2)) * scale
    back_odd = np.transpose(odd, (1, 0, 2)) * scale
    return [np.asarray(t, np.float32) for t in (even, odd, back_even, back_odd)]


def peers():
    rows, cols = lax.axis_size("row"), lax.axis_size("col")
    row, col = lax.axis_index("row"), lax.axis_index("col")
    result = []
    for step in range(1, rows * cols):
        r, c = row + step // cols, col + step % cols
        result.append((jnp.where(r >= rows, r - rows, r), jnp.where(c >= cols, c - cols, c)))
    return result


def own_index():
    return lax.axis_index("row") * lax.axis_size("col") + lax.axis_index("col")


def greet():
    barrier = pltpu.get_barrier_semaphore()
    for peer in peers():
        pl.semaphore_signal(barrier, inc=1, device_id=peer, device_id_type=MESH)
    return barrier


def to_all(source, land, send_sem, recv_sem):
    copies = []
    for n, peer in enumerate(peers()):
        copies.append(
            pltpu.make_async_remote_copy(
                src_ref=source(peer),
                dst_ref=land.at[own_index()],
                send_sem=send_sem.at[n],
                recv_sem=recv_sem.at[n],
                device_id=peer,
                device_id_type=MESH,
            )
        )
    return copies


def to_partner(source, land, send_sem, recv_sem):
    row = lax.axis_index("row")
    return pltpu.make_async_remote_copy(
        src_ref=source,
        dst_ref=land,
        send_sem=send_sem,
        recv_sem=recv_sem,
        device_id=(row + 1 - 2 * (row % 2), lax.axis_index("col")),
        device_id_type=MESH,
    )


def spectral_body(coeffs_ref, scalars, consts, out_ref, radius_ref, load_ref, scratch):
    even_ref, odd_ref, back_even_ref, back_odd_ref, fourier_ref, project_ref, weight_ref = consts
    field_scr, part_scr, line_scr, back_scr = scratch
    count, fields, degrees, width = coeffs_ref.shape
    half = degrees // 2
    level = lax.broadcasted_iota(jnp.int32, (degrees, width), 0)
    levelf = level.astype(F32)
    curve = levelf * (levelf + 1.0) * (1.0 / (degrees * degrees))
    viscous = (levelf + 2.0) * (6.0 / degrees)
    half_level = lax.broadcasted_iota(jnp.int32, (half, width), 0)
    even_order = lax.broadcasted_iota(jnp.int32, (half, width), 1) % 2 == 0

    for d in range(count):
        degree, tension, viscosity = scalars(d)
        keep = level <= degree
        shape = jnp.where(keep, coeffs_ref[d, 0], 0.0)
        field_scr[d, 0] = shape
        field_scr[d, 1] = shape * (tension * curve) + jnp.where(
            keep, coeffs_ref[d, 2] * (viscosity * viscous), 0.0
        )
        field_scr[d, 2] = jnp.where(keep, 3.0 * coeffs_ref[d, 1], 0.0)
        for f in range(3):
            low = field_scr[d, f, pl.ds(0, half, stride=2), :]
            high = field_scr[d, f, pl.ds(1, half, stride=2), :]
            part_scr[d, 2 * f] = jnp.where(even_order, low, high)
            part_scr[d, 2 * f + 1] = jnp.where(even_order, high, low)

    def synth(d, carry):
        total = [jnp.zeros((half, width), F32) for _ in range(6)]
        for i in range(half):
            pe, po = even_ref[i], odd_ref[i]
            for f in range(3):
                total[2 * f] = total[2 * f] + pe * part_scr[d, 2 * f, i : i + 1, :]
                total[2 * f + 1] = total[2 * f + 1] + po * part_scr[d, 2 * f + 1, i : i + 1, :]
        for f in range(3):
            for side in range(2):
                rows = total[2 * f] - total[2 * f + 1] if side else total[2 * f] + total[2 * f + 1]
                coarse = rows.astype(BF16)
                base = pl.multiple_of(((d * 3 + f) * 2 + side) * half, half)
                line_scr[pl.ds(base, half), :width] = coarse
                line_scr[pl.ds(base, half), width:] = (rows - coarse.astype(F32)).astype(BF16)
        return carry

    lax.fori_loop(0, count, synth, 0)
    for d in range(count):
        lines = line_scr[d * 3 * degrees : (d + 1) * 3 * degrees, :]
        surface = jnp.dot(lines, fourier_ref[...], preferred_element_type=F32)
        surface = surface[:, :width] + surface[:, width:]
        potential = surface[2 * degrees :]
        traction = surface[degrees : 2 * degrees] + 0.5 * potential * potential
        if radius_ref is not None:
            radius = jnp.exp(surface[:degrees])
            radius_ref[d] = radius
            load_ref[d] = traction * radius * radius * weight_ref[...]
        project = jnp.dot(traction.astype(BF16), project_ref[...], preferred_element_type=F32)
        back_scr[d, 0] = project[:half] + project[half:]
        back_scr[d, 1] = project[:half] - project[half:]
    pair = math.gcd(count, 2)

    def analyse(block, carry):
        total = [jnp.zeros((half, width), F32) for _ in range(2 * pair)]
        for j in range(half):
            pe, po = back_even_ref[j], back_odd_ref[j]
            for n in range(pair):
                d = block * pair + n
                total[2 * n] = total[2 * n] + pe * back_scr[d, 0, j : j + 1, :]
                total[2 * n + 1] = total[2 * n + 1] + po * back_scr[d, 1, j : j + 1, :]
        for n in range(pair):
            d = block * pair + n
            degree = scalars(d)[0]
            low, high = total[2 * n], total[2 * n + 1]
            out_ref[d, pl.ds(0, half, stride=2), :] = jnp.where(
                2 * half_level <= degree, jnp.where(even_order, low, high), 0.0
            )
            out_ref[d, pl.ds(1, half, stride=2), :] = jnp.where(
                2 * half_level + 1 <= degree, jnp.where(even_order, high, low), 0.0
            )
        return carry

    lax.fori_loop(0, count // pair, analyse, 0)


def spectral_kernel(
    degree_ref, material_ref, split_material_ref, coeffs_ref, all_coeffs_ref, split_ref, basis_ref,
    *rest,
):
    consts, rest = rest[:7], rest[7:]
    out_ref, radius_ref, load_ref, split_out_ref, points_ref = rest[:5]
    scratch, rest = rest[5:9], rest[9:]
    (shape_scr, point_scr, send_scr, land_scr, give_scr, came_scr, full_scr,
     local_sem, send_sem, recv_sem, give_sem, came_sem) = rest
    count, fields, degrees, width = coeffs_ref.shape
    drops = shape_scr.shape[0]
    split_count, half_width = split_ref.shape[0], split_ref.shape[3]
    share, orders = split_count // 2, half_width // 2
    devices = land_scr.shape[0]
    steps = drops // count
    step = pl.program_id(0)
    row, col = lax.axis_index("row"), lax.axis_index("col")
    parity = row % 2
    local = pltpu.make_async_copy(all_coeffs_ref.at[:, 0], shape_scr, local_sem)
    swap = to_partner(give_scr, came_scr, give_sem, came_sem)

    @pl.when(step == 0)
    def _():
        local.start()
        greet()
        give_scr[...] = split_ref[pl.ds((1 - parity) * share, share)].astype(BF16)

    @pl.when(step < steps)
    def _():
        first = step * count

        def scalars(d):
            at = first + d
            return degree_ref[at], material_ref[0, at], material_ref[1, at]

        spectral_body(coeffs_ref, scalars, consts, out_ref, radius_ref, load_ref, scratch)

    @pl.when(step == 0)
    def _():
        local.wait()
        level = lax.broadcasted_iota(jnp.int32, (degrees, width), 0)
        point_count = basis_ref.shape[0]
        for d in range(drops):
            shape = jnp.where(level <= degree_ref[d], shape_scr[d], 0.0)
            for p in range(point_count):
                point_scr[p, d : d + 1, :] = jnp.sum(shape * basis_ref[p], axis=0, keepdims=True)
        lane = lax.broadcasted_iota(jnp.int32, (drops, LANES), 1)
        surface = jnp.zeros((drops, LANES), F32)
        for p in range(point_count):
            surface = jnp.where(lane == p, jnp.sum(point_scr[p], axis=1, keepdims=True), surface)
        send_scr[...] = jnp.exp(surface).astype(BF16)
        pl.semaphore_wait(pltpu.get_barrier_semaphore(), devices - 1)
        swap.start()
        for copy in to_all(lambda peer: send_scr, land_scr, send_sem, recv_sem):
            copy.start()
        land_scr[own_index()] = send_scr[...]

    @pl.when(step == steps)
    def _():
        swap.wait()
        mine = split_ref[pl.ds(parity * share, share)]
        came = came_scr[...].astype(F32)
        for d in range(share):
            for f in range(fields):
                lower = jnp.where(parity == 0, mine[d, f], came[d, f])
                upper = jnp.where(parity == 0, came[d, f], mine[d, f])
                full_scr[d, f] = jnp.concatenate(
                    [lower[:, :orders], upper[:, :orders], lower[:, orders:], upper[:, orders:]],
                    axis=1,
                )
        start = (row // 2 * lax.axis_size("col") + col) * split_count + parity * share

        def scalars(d):
            at = start + d
            return degrees - 1, split_material_ref[0, at], split_material_ref[1, at]

        spectral_body(full_scr, scalars, consts, split_out_ref, None, None, scratch)
        for copy in to_all(lambda peer: send_scr, land_scr, send_sem, recv_sem):
            copy.wait()
        points_ref[...] = land_scr[...]


def spectral(coeffs, degree, material, split_coeffs, split_material, basis, tables, devices):
    drops, fields, degrees, width = coeffs.shape
    split_count, half_width = split_coeffs.shape[0], split_coeffs.shape[3]
    share = split_count // 2
    legendre, fourier, weight, sine, cosine, lon = tables
    half = degrees // 2
    block = math.gcd(drops, 4)
    steps = drops // block
    exact = np.asarray(fourier, np.float32)
    coarse = exact.astype(ml_dtypes.bfloat16)
    fine = (exact - coarse.astype(np.float32)).astype(ml_dtypes.bfloat16)
    fourier_parts = jnp.asarray(np.block([[coarse, fine], [coarse, np.zeros_like(fine)]]))
    project = jnp.asarray(np.ascontiguousarray(coarse.T))
    folded = np.concatenate([weight[:half], weight[:half]]) / (8.0 * math.pi)
    weight_grid = jnp.asarray(np.broadcast_to(folded[:, None], (degrees, width)), F32)
    parity = [jnp.asarray(t) for t in parity_tables(legendre, weight)]
    smem = pl.BlockSpec(memory_space=pltpu.SMEM)
    vmem = pl.BlockSpec(memory_space=pltpu.VMEM)
    consts = parity + [fourier_parts, project, weight_grid]
    at = lambda i: jnp.minimum(i, steps - 1)
    grid_spec = pl.BlockSpec((block, degrees, width), lambda i: (at(i), 0, 0))
    grid_shape = jax.ShapeDtypeStruct((drops, degrees, width), F32)
    held = (share, fields, degrees, half_width)
    return pl.pallas_call(
        spectral_kernel,
        grid=(steps + 1,),
        in_specs=[
            smem, smem, smem,
            pl.BlockSpec((block, fields, degrees, width), lambda i: (at(i), 0, 0, 0)),
            pl.BlockSpec(memory_space=pl.ANY), vmem, vmem,
        ]
        + [vmem] * len(consts),
        out_specs=[grid_spec] * 3 + [vmem, vmem],
        out_shape=[grid_shape] * 3
        + [
            jax.ShapeDtypeStruct((share, degrees, width), F32),
            jax.ShapeDtypeStruct((devices, drops, LANES), BF16),
        ],
        scratch_shapes=[
            pltpu.VMEM((block, 3, degrees, width), F32),
            pltpu.VMEM((block, 6, half, width), F32),
            pltpu.VMEM((block * 3 * degrees, 2 * width), BF16),
            pltpu.VMEM((block, 2, half, width), F32),
            pltpu.VMEM((drops, degrees, width), F32),
            pltpu.VMEM((basis.shape[0], drops, width), F32),
            pltpu.VMEM((drops, LANES), BF16),
            pltpu.VMEM((devices, drops, LANES), BF16),
            pltpu.VMEM(held, BF16),
            pltpu.VMEM(held, BF16),
            pltpu.VMEM((share, fields, degrees, width), F32),
            pltpu.SemaphoreType.DMA,
            pltpu.SemaphoreType.DMA((devices,)),
            pltpu.SemaphoreType.DMA((devices,)),
            pltpu.SemaphoreType.DMA,
            pltpu.SemaphoreType.DMA,
        ],
        compiler_params=pltpu.CompilerParams(
            collective_id=0, has_side_effects=True, vmem_limit_bytes=VMEM_BYTES
        ),
    )(
        degree, material.T, split_material.T, coeffs, coeffs, split_coeffs, basis, *consts
    )


def near_kernel(
    normals, dev_ref, slot_ref, sep_ref, points_ref, radius_ref, load_ref, split_ref,
    turn_ref, tilt_ref, out_ref, split_out_ref,
    entry_ref, target_scr, spread_scr, total_scr, send_scr, land_scr, give_scr, came_scr,
    send_sem, recv_sem, give_sem, came_sem,
):
    drops, degrees, width = radius_ref.shape
    devices = land_scr.shape[0]
    me = own_index()
    barrier = greet()
    readers = dev_ref.shape[0]
    entries = drops * readers
    entry_lane = lax.broadcasted_iota(jnp.int32, (readers, LANES), 1)
    for d in range(drops):
        columns_of = [sep_ref[c, :, d : d + 1] for c in range(3)]
        columns_of += [ref[:, d : d + 1].astype(F32) for ref in (dev_ref, slot_ref)]
        rows_of = jnp.zeros((readers, LANES), F32)
        for n, column in enumerate(columns_of):
            rows_of = jnp.where(entry_lane == n, column, rows_of)
        entry_ref[d * readers : (d + 1) * readers, :] = rows_of
    share, split_width = split_ref.shape[0], split_ref.shape[2]
    orders = split_width // 4
    parity = lax.axis_index("row") % 2
    for n in range(share):
        whole = split_ref[n]
        cut = [whole[:, k * orders : (k + 1) * orders] for k in range(4)]
        lower = jnp.concatenate([cut[0], cut[2]], axis=1)
        upper = jnp.concatenate([cut[1], cut[3]], axis=1)
        give_scr[n] = jnp.where(parity == 0, upper, lower).astype(BF16)
        split_out_ref[parity * share + n] = jnp.where(parity == 0, lower, upper)
    swap = to_partner(give_scr, came_scr, give_sem, came_sem)
    half = degrees // 2
    targets = points_ref.shape[0]
    columns = spread_scr.shape[1]
    point_count = len(normals)
    to = entry_ref[:, 3:4].astype(jnp.int32)
    slot = entry_ref[:, 4:5].astype(jnp.int32)
    pick = lax.broadcasted_iota(jnp.int32, (entries, targets), 1) == to * drops + slot
    target_scr[...] = jnp.dot(
        pick.astype(F32).astype(BF16), points_ref[...], preferred_element_type=F32
    )
    lane = lax.broadcasted_iota(jnp.int32, (readers, columns), 1)
    block = drops * point_count
    kind = lane // block * point_count + lane % point_count
    lane_slot = lane % block // point_count

    def one_drop(d, carry):
        rows = pl.ds(pl.multiple_of(d * readers, readers), readers)
        sep = entry_ref[rows, :]
        reach = target_scr[rows, :]
        xs, ring, height, square = [], [], [], []
        for p in range(point_count):
            at = reach[:, p : p + 1]
            x = [
                jnp.broadcast_to(sep[:, c : c + 1] + at * normals[p][c], (readers, width))
                for c in range(3)
            ]
            xs.append(x)
            ring.append(x[0] * turn_ref[0:1, :] + x[1] * turn_ref[1:2, :])
            height.append(x[2])
            square.append(x[0] * x[0] + x[1] * x[1] + x[2] * x[2] + SOFTENING)

        def cell(a, r, rr, h, sq):
            off = a - r
            m = r * off
            t = (sq - rr) - m
            rho = t - m
            inv = lax.rsqrt(rho)
            g = (inv * h) * (inv * inv)
            return g * ((rho - m) + SOFTENING), g * off

        def tile(points, jt, acc):
            acc = list(acc)
            base = pl.multiple_of(jt * 8, 8)
            for q in range(8):
                j = base + q
                r0 = radius_ref[d, pl.ds(j, 1), :]
                r1 = radius_ref[d, pl.ds(j + half, 1), :]
                h0 = load_ref[d, pl.ds(j, 1), :]
                h1 = load_ref[d, pl.ds(j + half, 1), :]
                s = tilt_ref[0, pl.ds(j, 1), :]
                c = tilt_ref[1, pl.ds(j, 1), :]
                q0, q1 = r0 * r0, r1 * r1
                for n, p in enumerate(points):
                    flat = s * ring[p]
                    up = c * height[p]
                    w0, v0 = cell(flat + up, r0, q0, h0, square[p])
                    w1, v1 = cell(flat - up, r1, q1, h1, square[p])
                    acc[3 * n] = acc[3 * n] + s * (w0 + w1)
                    acc[3 * n + 1] = acc[3 * n + 1] + c * (w0 - w1)
                    acc[3 * n + 2] = acc[3 * n + 2] + (v0 + v1)
            return tuple(acc)

        zero = jnp.zeros((readers, width), F32)
        acc = ()
        for low in range(0, point_count, 2):
            points = range(low, min(low + 2, point_count))
            acc += lax.fori_loop(
                0, half // 8, functools.partial(tile, points), (zero,) * (3 * len(points))
            )
        spread = jnp.zeros((readers, columns), F32)
        for p in range(point_count):
            around, up, along = acc[3 * p : 3 * p + 3]
            terms = (around * turn_ref[0:1, :], around * turn_ref[1:2, :], up)
            for c in range(3):
                value = jnp.sum(terms[c] + along * xs[p][c], axis=1, keepdims=True)
                spread = jnp.where(kind == c * point_count + p, value, spread)
        spread_scr[rows, :] = jnp.where(
            lane_slot == sep[:, 4:5].astype(jnp.int32), spread, 0.0
        )
        return carry

    lax.fori_loop(0, drops // 2, one_drop, 0)
    pl.semaphore_wait(barrier, devices - 1)
    swap.start()
    lax.fori_loop(drops // 2, drops, one_drop, 0)
    goes = lax.broadcasted_iota(jnp.int32, (entries, devices), 1) == to
    goes = goes.astype(F32).astype(BF16)
    spread = spread_scr[...]
    coarse = spread.astype(BF16)
    fine = (spread - coarse.astype(F32)).astype(BF16)
    first = (((0,), (0,)), ((), ()))
    total_scr[...] = lax.dot_general(
        goes, coarse, first, preferred_element_type=F32
    ) + lax.dot_general(goes, fine, first, preferred_element_type=F32)

    for device in range(devices):
        send_scr[device] = total_scr[device : device + 1, :]
    col_count = lax.axis_size("col")
    copies = to_all(
        lambda peer: send_scr.at[peer[0] * col_count + peer[1]], land_scr, send_sem, recv_sem
    )
    for copy in copies:
        copy.start()
    land_scr[me] = send_scr[me]
    swap.wait()
    split_out_ref[pl.ds((1 - parity) * share, share)] = came_scr[...].astype(F32)
    for copy in copies:
        copy.wait()
    velocity = jnp.sum(land_scr[...], axis=0)
    for c in range(3):
        out_ref[c : c + 1, :] = velocity[:, c * block : (c + 1) * block]


def near(dev, slot, sep, points, radius, load, split_out, tables, normals, devices, columns):
    legendre, fourier, weight, sine, cosine, lon = tables
    drops, degrees, width = radius.shape
    share = split_out.shape[0]
    half = degrees // 2
    turn = jnp.asarray(np.stack([np.cos(lon), np.sin(lon)]), F32)
    tilt = np.stack([sine[:half], cosine[:half]])
    tilt = jnp.asarray(np.broadcast_to(tilt[:, :, None], (2, half, width)), F32)
    entries = drops * dev.shape[0]
    vmem = pl.BlockSpec(memory_space=pltpu.VMEM)
    held = (share, degrees, width // 2)
    return pl.pallas_call(
        functools.partial(near_kernel, normals),
        in_specs=[vmem] * 9,
        out_specs=[vmem, vmem],
        out_shape=[
            jax.ShapeDtypeStruct((3, drops * len(normals)), F32),
            jax.ShapeDtypeStruct((2 * share, degrees, width // 2), F32),
        ],
        scratch_shapes=[
            pltpu.VMEM((entries, LANES), F32),
            pltpu.VMEM((entries, LANES), F32),
            pltpu.VMEM((entries, columns), F32),
            pltpu.VMEM((devices, columns), F32),
            pltpu.VMEM((devices, 1, columns), F32),
            pltpu.VMEM((devices, 1, columns), F32),
            pltpu.VMEM(held, BF16),
            pltpu.VMEM(held, BF16),
            pltpu.SemaphoreType.DMA((devices,)),
            pltpu.SemaphoreType.DMA((devices,)),
            pltpu.SemaphoreType.DMA,
            pltpu.SemaphoreType.DMA,
        ],
        compiler_params=pltpu.CompilerParams(
            collective_id=1, has_side_effects=True, vmem_limit_bytes=VMEM_BYTES
        ),
        cost_estimate=pl.CostEstimate(
            flops=entries * 4 * 8192 * 20, bytes_accessed=2_000_000, transcendentals=entries * 32768
        ),
    )(dev, slot, sep, points, radius, load, split_out, turn, tilt)


def per_device(
    coeffs, degree, material, split_coeffs, split_material, separation, reader_dev, reader_slot
):
    drops, fields, degrees, width = coeffs.shape
    row_count, col_count = lax.axis_size("row"), lax.axis_size("col")
    devices = row_count * col_count
    tables = spectral_tables(degrees)
    legendre, fourier, weight, sine, cosine, lon = tables
    nlat, nlon = degrees, 2 * degrees

    lat_points = range(nlat // 4, nlat, nlat // 2)
    lon_points = range(0, nlon, nlon // 2)
    spots = [(j, k) for j in lat_points for k in lon_points]
    normals = [
        (
            float(sine[j] * math.cos(lon[k])),
            float(sine[j] * math.sin(lon[k])),
            float(cosine[j]),
        )
        for j, k in spots
    ]
    order = np.arange(width) % degrees
    basis = jnp.asarray(
        np.stack([legendre[order, j, :].T * fourier[:, k][None, :] for j, k in spots]), F32
    )
    traction_coeffs, radius, load, split_out, points = spectral(
        coeffs, degree, material, split_coeffs, split_material, basis, tables, devices
    )
    point_count = len(spots)
    columns = -(-3 * drops * point_count // LANES) * LANES
    velocity, split_traction = near(
        reader_dev.T, reader_slot.T, jnp.transpose(separation, (0, 2, 1)),
        points.reshape(devices * drops, LANES), radius, load, split_out,
        tables, normals, devices, columns,
    )
    return traction_coeffs, split_traction, velocity


def solution(mesh):
    both = ("row", "col")
    in_specs = (
        P(both, None, None, None),
        P(both),
        P(both, None),
        P(both, None, None, None),
        P(),
        P(None, both, None),
        P(both, None),
        P(both, None),
    )
    out_specs = (P(both, None, None), P(both, None, None), P(None, both))
    return jax.shard_map(
        per_device, mesh=mesh, in_specs=in_specs, out_specs=out_specs, check_vma=False
    )
```

```python
import functools
import math

import jax
import jax.numpy as jnp
import ml_dtypes
import numpy as np
from jax import lax
from jax.experimental import pallas as pl
from jax.experimental.pallas import tpu as pltpu
from jax.sharding import PartitionSpec as P

SOFTENING = 0.04
VMEM_BYTES = 60 << 20
LANES = 128
F32 = jnp.float32
BF16 = jnp.bfloat16
MESH = pl.DeviceIdType.MESH


def spectral_tables(degrees):
    nlon = 2 * degrees
    theta = (np.arange(degrees) + 0.5) * (math.pi / degrees)
    cosine, sine = np.cos(theta), np.sin(theta)
    legendre = np.zeros((degrees, degrees, degrees))
    for order in range(degrees):
        total = sum(math.log((2.0 * i + 1.0) / (2.0 * i)) for i in range(1, order + 1))
        older = np.exp(0.5 * total + order * np.log(sine)) / math.sqrt(4.0 * math.pi)
        legendre[order, :, order] = older
        if order + 1 < degrees:
            newer = math.sqrt(2.0 * order + 3.0) * cosine * older
            legendre[order, :, order + 1] = newer
            for l in range(order + 2, degrees):
                a = math.sqrt((4.0 * l * l - 1.0) / (l * l - order * order))
                b = math.sqrt(((l - 1.0) ** 2 - order * order) / (4.0 * (l - 1.0) ** 2 - 1.0))
                older, newer = newer, a * (cosine * newer - b * older)
                legendre[order, :, l] = newer
    phase = np.arange(degrees)[:, None] * np.arange(nlon)[None, :] % nlon * (2.0 * math.pi / nlon)
    fourier = np.concatenate([np.cos(phase), np.sin(phase)], axis=0)
    weight = sine * (math.pi / degrees) * (2.0 * math.pi / nlon)
    lon = np.arange(nlon) * (2.0 * math.pi / nlon)
    return legendre, fourier, weight, sine, cosine, lon


def parity_tables(legendre, weight):
    degrees = legendre.shape[0]
    half = degrees // 2
    order = np.arange(2 * degrees) % degrees
    by_lane = legendre[order]
    step = np.arange(half)
    even = np.zeros((half, half, 2 * degrees))
    odd = np.zeros((half, half, 2 * degrees))
    for lane, m in enumerate(order):
        even[:, :, lane] = by_lane[lane][:half, 2 * step + m % 2].T
        odd[:, :, lane] = by_lane[lane][:half, 2 * step + 1 - m % 2].T
    scale = weight[:half, None, None]
    back_even = np.transpose(even, (1, 0, 2)) * scale
    back_odd = np.transpose(odd, (1, 0, 2)) * scale
    return [np.asarray(t, np.float32) for t in (even, odd, back_even, back_odd)]


def peers():
    rows, cols = lax.axis_size("row"), lax.axis_size("col")
    row, col = lax.axis_index("row"), lax.axis_index("col")
    result = []
    for step in range(1, rows * cols):
        r, c = row + step // cols, col + step % cols
        result.append((jnp.where(r >= rows, r - rows, r), jnp.where(c >= cols, c - cols, c)))
    return result


def own_index():
    return lax.axis_index("row") * lax.axis_size("col") + lax.axis_index("col")


def greet():
    barrier = pltpu.get_barrier_semaphore()
    for peer in peers():
        pl.semaphore_signal(barrier, inc=1, device_id=peer, device_id_type=MESH)
    return barrier


def to_all(source, land, send_sem, recv_sem):
    copies = []
    for n, peer in enumerate(peers()):
        copies.append(
            pltpu.make_async_remote_copy(
                src_ref=source(peer),
                dst_ref=land.at[own_index()],
                send_sem=send_sem.at[n],
                recv_sem=recv_sem.at[n],
                device_id=peer,
                device_id_type=MESH,
            )
        )
    return copies


def to_partner(source, land, send_sem, recv_sem):
    row = lax.axis_index("row")
    return pltpu.make_async_remote_copy(
        src_ref=source,
        dst_ref=land,
        send_sem=send_sem,
        recv_sem=recv_sem,
        device_id=(row + 1 - 2 * (row % 2), lax.axis_index("col")),
        device_id_type=MESH,
    )


def spectral_body(coeffs_ref, scalars, consts, out_ref, radius_ref, load_ref, scratch):
    even_ref, odd_ref, back_even_ref, back_odd_ref, fourier_ref, project_ref, weight_ref = consts
    field_scr, part_scr, line_scr, back_scr = scratch
    count, fields, degrees, width = coeffs_ref.shape
    half = degrees // 2
    level = lax.broadcasted_iota(jnp.int32, (degrees, width), 0)
    levelf = level.astype(F32)
    curve = levelf * (levelf + 1.0) * (1.0 / (degrees * degrees))
    viscous = (levelf + 2.0) * (6.0 / degrees)
    half_level = lax.broadcasted_iota(jnp.int32, (half, width), 0)
    even_order = lax.broadcasted_iota(jnp.int32, (half, width), 1) % 2 == 0

    for d in range(count):
        degree, tension, viscosity = scalars(d)
        keep = level <= degree
        shape = jnp.where(keep, coeffs_ref[d, 0], 0.0)
        field_scr[d, 0] = shape
        field_scr[d, 1] = shape * (tension * curve) + jnp.where(
            keep, coeffs_ref[d, 2] * (viscosity * viscous), 0.0
        )
        field_scr[d, 2] = jnp.where(keep, 3.0 * coeffs_ref[d, 1], 0.0)
        for f in range(3):
            low = field_scr[d, f, pl.ds(0, half, stride=2), :]
            high = field_scr[d, f, pl.ds(1, half, stride=2), :]
            part_scr[d, 2 * f] = jnp.where(even_order, low, high)
            part_scr[d, 2 * f + 1] = jnp.where(even_order, high, low)

    def synth(d, carry):
        total = [jnp.zeros((half, width), F32) for _ in range(6)]
        for i in range(half):
            pe, po = even_ref[i], odd_ref[i]
            for f in range(3):
                total[2 * f] = total[2 * f] + pe * part_scr[d, 2 * f, i : i + 1, :]
                total[2 * f + 1] = total[2 * f + 1] + po * part_scr[d, 2 * f + 1, i : i + 1, :]
        for f in range(3):
            for side in range(2):
                rows = total[2 * f] - total[2 * f + 1] if side else total[2 * f] + total[2 * f + 1]
                coarse = rows.astype(BF16)
                base = pl.multiple_of(((d * 3 + f) * 2 + side) * half, half)
                line_scr[pl.ds(base, half), :width] = coarse
                line_scr[pl.ds(base, half), width:] = (rows - coarse.astype(F32)).astype(BF16)
        return carry

    lax.fori_loop(0, count, synth, 0)
    for d in range(count):
        lines = line_scr[d * 3 * degrees : (d + 1) * 3 * degrees, :]
        surface = jnp.dot(lines, fourier_ref[...], preferred_element_type=F32)
        surface = surface[:, :width] + surface[:, width:]
        potential = surface[2 * degrees :]
        traction = surface[degrees : 2 * degrees] + 0.5 * potential * potential
        if radius_ref is not None:
            radius = jnp.exp(surface[:degrees])
            radius_ref[d] = radius
            load_ref[d] = traction * radius * radius * weight_ref[...]
        project = jnp.dot(traction.astype(BF16), project_ref[...], preferred_element_type=F32)
        back_scr[d, 0] = project[:half] + project[half:]
        back_scr[d, 1] = project[:half] - project[half:]
    pair = math.gcd(count, 2)

    def analyse(block, carry):
        total = [jnp.zeros((half, width), F32) for _ in range(2 * pair)]
        for j in range(half):
            pe, po = back_even_ref[j], back_odd_ref[j]
            for n in range(pair):
                d = block * pair + n
                total[2 * n] = total[2 * n] + pe * back_scr[d, 0, j : j + 1, :]
                total[2 * n + 1] = total[2 * n + 1] + po * back_scr[d, 1, j : j + 1, :]
        for n in range(pair):
            d = block * pair + n
            degree = scalars(d)[0]
            low, high = total[2 * n], total[2 * n + 1]
            out_ref[d, pl.ds(0, half, stride=2), :] = jnp.where(
                2 * half_level <= degree, jnp.where(even_order, low, high), 0.0
            )
            out_ref[d, pl.ds(1, half, stride=2), :] = jnp.where(
                2 * half_level + 1 <= degree, jnp.where(even_order, high, low), 0.0
            )
        return carry

    lax.fori_loop(0, count // pair, analyse, 0)


def spectral_kernel(
    degree_ref, material_ref, split_material_ref, coeffs_ref, all_coeffs_ref, split_ref, basis_ref,
    *rest,
):
    consts, rest = rest[:7], rest[7:]
    out_ref, radius_ref, load_ref, split_out_ref, points_ref = rest[:5]
    scratch, rest = rest[5:9], rest[9:]
    (shape_scr, point_scr, send_scr, land_scr, give_scr, came_scr, full_scr,
     local_sem, send_sem, recv_sem, give_sem, came_sem) = rest
    count, fields, degrees, width = coeffs_ref.shape
    drops = shape_scr.shape[0]
    split_count, half_width = split_ref.shape[0], split_ref.shape[3]
    share, orders = split_count // 2, half_width // 2
    devices = land_scr.shape[0]
    steps = drops // count
    step = pl.program_id(0)
    row, col = lax.axis_index("row"), lax.axis_index("col")
    parity = row % 2
    local = pltpu.make_async_copy(all_coeffs_ref.at[:, 0], shape_scr, local_sem)
    swap = to_partner(give_scr, came_scr, give_sem, came_sem)

    @pl.when(step == 0)
    def _():
        local.start()
        greet()
        give_scr[...] = split_ref[pl.ds((1 - parity) * share, share)].astype(BF16)

    @pl.when(step < steps)
    def _():
        first = step * count

        def scalars(d):
            at = first + d
            return degree_ref[at], material_ref[0, at], material_ref[1, at]

        spectral_body(coeffs_ref, scalars, consts, out_ref, radius_ref, load_ref, scratch)

    @pl.when(step == 0)
    def _():
        local.wait()
        level = lax.broadcasted_iota(jnp.int32, (degrees, width), 0)
        point_count = basis_ref.shape[0]
        for d in range(drops):
            shape = jnp.where(level <= degree_ref[d], shape_scr[d], 0.0)
            for p in range(point_count):
                point_scr[p, d : d + 1, :] = jnp.sum(shape * basis_ref[p], axis=0, keepdims=True)
        lane = lax.broadcasted_iota(jnp.int32, (drops, LANES), 1)
        surface = jnp.zeros((drops, LANES), F32)
        for p in range(point_count):
            surface = jnp.where(lane == p, jnp.sum(point_scr[p], axis=1, keepdims=True), surface)
        send_scr[...] = jnp.exp(surface).astype(BF16)
        pl.semaphore_wait(pltpu.get_barrier_semaphore(), devices - 1)
        swap.start()
        for copy in to_all(lambda peer: send_scr, land_scr, send_sem, recv_sem):
            copy.start()
        land_scr[own_index()] = send_scr[...]

    @pl.when(step == steps)
    def _():
        swap.wait()
        mine = split_ref[pl.ds(parity * share, share)]
        came = came_scr[...].astype(F32)
        for d in range(share):
            for f in range(fields):
                lower = jnp.where(parity == 0, mine[d, f], came[d, f])
                upper = jnp.where(parity == 0, came[d, f], mine[d, f])
                full_scr[d, f] = jnp.concatenate(
                    [lower[:, :orders], upper[:, :orders], lower[:, orders:], upper[:, orders:]],
                    axis=1,
                )
        start = (row // 2 * lax.axis_size("col") + col) * split_count + parity * share

        def scalars(d):
            at = start + d
            return degrees - 1, split_material_ref[0, at], split_material_ref[1, at]

        spectral_body(full_scr, scalars, consts, split_out_ref, None, None, scratch)
        for copy in to_all(lambda peer: send_scr, land_scr, send_sem, recv_sem):
            copy.wait()
        points_ref[...] = land_scr[...]


def spectral(coeffs, degree, material, split_coeffs, split_material, basis, tables, devices):
    drops, fields, degrees, width = coeffs.shape
    split_count, half_width = split_coeffs.shape[0], split_coeffs.shape[3]
    share = split_count // 2
    legendre, fourier, weight, sine, cosine, lon = tables
    half = degrees // 2
    block = math.gcd(drops, 4)
    steps = drops // block
    exact = np.asarray(fourier, np.float32)
    coarse = exact.astype(ml_dtypes.bfloat16)
    fine = (exact - coarse.astype(np.float32)).astype(ml_dtypes.bfloat16)
    fourier_parts = jnp.asarray(np.block([[coarse, fine], [coarse, np.zeros_like(fine)]]))
    project = jnp.asarray(np.ascontiguousarray(coarse.T))
    folded = np.concatenate([weight[:half], weight[:half]]) / (8.0 * math.pi)
    weight_grid = jnp.asarray(np.broadcast_to(folded[:, None], (degrees, width)), F32)
    parity = [jnp.asarray(t) for t in parity_tables(legendre, weight)]
    smem = pl.BlockSpec(memory_space=pltpu.SMEM)
    vmem = pl.BlockSpec(memory_space=pltpu.VMEM)
    consts = parity + [fourier_parts, project, weight_grid]
    at = lambda i: jnp.minimum(i, steps - 1)
    grid_spec = pl.BlockSpec((block, degrees, width), lambda i: (at(i), 0, 0))
    grid_shape = jax.ShapeDtypeStruct((drops, degrees, width), F32)
    held = (share, fields, degrees, half_width)
    return pl.pallas_call(
        spectral_kernel,
        grid=(steps + 1,),
        in_specs=[
            smem, smem, smem,
            pl.BlockSpec((block, fields, degrees, width), lambda i: (at(i), 0, 0, 0)),
            pl.BlockSpec(memory_space=pl.ANY), vmem, vmem,
        ]
        + [vmem] * len(consts),
        out_specs=[grid_spec] * 3 + [vmem, vmem],
        out_shape=[grid_shape] * 3
        + [
            jax.ShapeDtypeStruct((share, degrees, width), F32),
            jax.ShapeDtypeStruct((devices, drops, LANES), BF16),
        ],
        scratch_shapes=[
            pltpu.VMEM((block, 3, degrees, width), F32),
            pltpu.VMEM((block, 6, half, width), F32),
            pltpu.VMEM((block * 3 * degrees, 2 * width), BF16),
            pltpu.VMEM((block, 2, half, width), F32),
            pltpu.VMEM((drops, degrees, width), F32),
            pltpu.VMEM((basis.shape[0], drops, width), F32),
            pltpu.VMEM((drops, LANES), BF16),
            pltpu.VMEM((devices, drops, LANES), BF16),
            pltpu.VMEM(held, BF16),
            pltpu.VMEM(held, BF16),
            pltpu.VMEM((share, fields, degrees, width), F32),
            pltpu.SemaphoreType.DMA,
            pltpu.SemaphoreType.DMA((devices,)),
            pltpu.SemaphoreType.DMA((devices,)),
            pltpu.SemaphoreType.DMA,
            pltpu.SemaphoreType.DMA,
        ],
        compiler_params=pltpu.CompilerParams(
            collective_id=0, has_side_effects=True, vmem_limit_bytes=VMEM_BYTES
        ),
    )(
        degree, material.T, split_material.T, coeffs, coeffs, split_coeffs, basis, *consts
    )


def near_kernel(
    normals, dev_ref, slot_ref, sep_ref, points_ref, radius_ref, load_ref, split_ref,
    turn_ref, tilt_ref, out_ref, split_out_ref,
    entry_ref, target_scr, spread_scr, total_scr, send_scr, land_scr, give_scr, came_scr,
    send_sem, recv_sem, give_sem, came_sem,
):
    drops, degrees, width = radius_ref.shape
    devices = land_scr.shape[0]
    me = own_index()
    barrier = greet()
    readers = dev_ref.shape[0]
    entries = drops * readers
    entry_lane = lax.broadcasted_iota(jnp.int32, (readers, LANES), 1)
    for d in range(drops):
        columns_of = [sep_ref[c, :, d : d + 1] for c in range(3)]
        columns_of += [ref[:, d : d + 1].astype(F32) for ref in (dev_ref, slot_ref)]
        rows_of = jnp.zeros((readers, LANES), F32)
        for n, column in enumerate(columns_of):
            rows_of = jnp.where(entry_lane == n, column, rows_of)
        entry_ref[d * readers : (d + 1) * readers, :] = rows_of
    share, split_width = split_ref.shape[0], split_ref.shape[2]
    orders = split_width // 4
    parity = lax.axis_index("row") % 2
    for n in range(share):
        whole = split_ref[n]
        cut = [whole[:, k * orders : (k + 1) * orders] for k in range(4)]
        lower = jnp.concatenate([cut[0], cut[2]], axis=1)
        upper = jnp.concatenate([cut[1], cut[3]], axis=1)
        give_scr[n] = jnp.where(parity == 0, upper, lower).astype(BF16)
        split_out_ref[parity * share + n] = jnp.where(parity == 0, lower, upper)
    swap = to_partner(give_scr, came_scr, give_sem, came_sem)
    half = degrees // 2
    targets = points_ref.shape[0]
    columns = spread_scr.shape[1]
    point_count = len(normals)
    to = entry_ref[:, 3:4].astype(jnp.int32)
    slot = entry_ref[:, 4:5].astype(jnp.int32)
    pick = lax.broadcasted_iota(jnp.int32, (entries, targets), 1) == to * drops + slot
    target_scr[...] = jnp.dot(
        pick.astype(F32).astype(BF16), points_ref[...], preferred_element_type=F32
    )
    lane = lax.broadcasted_iota(jnp.int32, (readers, columns), 1)
    block = drops * point_count
    kind = lane // block * point_count + lane % point_count
    lane_slot = lane % block // point_count

    def one_drop(d, carry):
        rows = pl.ds(pl.multiple_of(d * readers, readers), readers)
        sep = entry_ref[rows, :]
        reach = target_scr[rows, :]
        xs, ring, height, square = [], [], [], []
        for p in range(point_count):
            at = reach[:, p : p + 1]
            x = [
                jnp.broadcast_to(sep[:, c : c + 1] + at * normals[p][c], (readers, width))
                for c in range(3)
            ]
            xs.append(x)
            ring.append(x[0] * turn_ref[0:1, :] + x[1] * turn_ref[1:2, :])
            height.append(x[2])
            square.append(x[0] * x[0] + x[1] * x[1] + x[2] * x[2] + SOFTENING)

        def cell(a, r, rr, h, sq):
            off = a - r
            m = r * off
            t = (sq - rr) - m
            rho = t - m
            inv = lax.rsqrt(rho)
            g = (inv * h) * (inv * inv)
            return g * ((rho - m) + SOFTENING), g * off

        def tile(points, jt, acc):
            acc = list(acc)
            base = pl.multiple_of(jt * 8, 8)
            for q in range(8):
                j = base + q
                r0 = radius_ref[d, pl.ds(j, 1), :]
                r1 = radius_ref[d, pl.ds(j + half, 1), :]
                h0 = load_ref[d, pl.ds(j, 1), :]
                h1 = load_ref[d, pl.ds(j + half, 1), :]
                s = tilt_ref[0, pl.ds(j, 1), :]
                c = tilt_ref[1, pl.ds(j, 1), :]
                q0, q1 = r0 * r0, r1 * r1
                for n, p in enumerate(points):
                    flat = s * ring[p]
                    up = c * height[p]
                    w0, v0 = cell(flat + up, r0, q0, h0, square[p])
                    w1, v1 = cell(flat - up, r1, q1, h1, square[p])
                    acc[3 * n] = acc[3 * n] + s * (w0 + w1)
                    acc[3 * n + 1] = acc[3 * n + 1] + c * (w0 - w1)
                    acc[3 * n + 2] = acc[3 * n + 2] + (v0 + v1)
            return tuple(acc)

        zero = jnp.zeros((readers, width), F32)
        acc = ()
        for low in range(0, point_count, 4):
            points = range(low, min(low + 4, point_count))
            acc += lax.fori_loop(
                0, half // 8, functools.partial(tile, points), (zero,) * (3 * len(points))
            )
        spread = jnp.zeros((readers, columns), F32)
        for p in range(point_count):
            around, up, along = acc[3 * p : 3 * p + 3]
            terms = (around * turn_ref[0:1, :], around * turn_ref[1:2, :], up)
            for c in range(3):
                value = jnp.sum(terms[c] + along * xs[p][c], axis=1, keepdims=True)
                spread = jnp.where(kind == c * point_count + p, value, spread)
        spread_scr[rows, :] = jnp.where(
            lane_slot == sep[:, 4:5].astype(jnp.int32), spread, 0.0
        )
        return carry

    lax.fori_loop(0, drops // 2, one_drop, 0)
    pl.semaphore_wait(barrier, devices - 1)
    swap.start()
    lax.fori_loop(drops // 2, drops, one_drop, 0)
    goes = lax.broadcasted_iota(jnp.int32, (entries, devices), 1) == to
    goes = goes.astype(F32).astype(BF16)
    spread = spread_scr[...]
    coarse = spread.astype(BF16)
    fine = (spread - coarse.astype(F32)).astype(BF16)
    first = (((0,), (0,)), ((), ()))
    total_scr[...] = lax.dot_general(
        goes, coarse, first, preferred_element_type=F32
    ) + lax.dot_general(goes, fine, first, preferred_element_type=F32)

    for device in range(devices):
        send_scr[device] = total_scr[device : device + 1, :]
    col_count = lax.axis_size("col")
    copies = to_all(
        lambda peer: send_scr.at[peer[0] * col_count + peer[1]], land_scr, send_sem, recv_sem
    )
    for copy in copies:
        copy.start()
    land_scr[me] = send_scr[me]
    swap.wait()
    split_out_ref[pl.ds((1 - parity) * share, share)] = came_scr[...].astype(F32)
    for copy in copies:
        copy.wait()
    velocity = jnp.sum(land_scr[...], axis=0)
    for c in range(3):
        out_ref[c : c + 1, :] = velocity[:, c * block : (c + 1) * block]


def near(dev, slot, sep, points, radius, load, split_out, tables, normals, devices, columns):
    legendre, fourier, weight, sine, cosine, lon = tables
    drops, degrees, width = radius.shape
    share = split_out.shape[0]
    half = degrees // 2
    turn = jnp.asarray(np.stack([np.cos(lon), np.sin(lon)]), F32)
    tilt = np.stack([sine[:half], cosine[:half]])
    tilt = jnp.asarray(np.broadcast_to(tilt[:, :, None], (2, half, width)), F32)
    entries = drops * dev.shape[0]
    vmem = pl.BlockSpec(memory_space=pltpu.VMEM)
    held = (share, degrees, width // 2)
    return pl.pallas_call(
        functools.partial(near_kernel, normals),
        in_specs=[vmem] * 9,
        out_specs=[vmem, vmem],
        out_shape=[
            jax.ShapeDtypeStruct((3, drops * len(normals)), F32),
            jax.ShapeDtypeStruct((2 * share, degrees, width // 2), F32),
        ],
        scratch_shapes=[
            pltpu.VMEM((entries, LANES), F32),
            pltpu.VMEM((entries, LANES), F32),
            pltpu.VMEM((entries, columns), F32),
            pltpu.VMEM((devices, columns), F32),
            pltpu.VMEM((devices, 1, columns), F32),
            pltpu.VMEM((devices, 1, columns), F32),
            pltpu.VMEM(held, BF16),
            pltpu.VMEM(held, BF16),
            pltpu.SemaphoreType.DMA((devices,)),
            pltpu.SemaphoreType.DMA((devices,)),
            pltpu.SemaphoreType.DMA,
            pltpu.SemaphoreType.DMA,
        ],
        compiler_params=pltpu.CompilerParams(
            collective_id=1, has_side_effects=True, vmem_limit_bytes=VMEM_BYTES
        ),
        cost_estimate=pl.CostEstimate(
            flops=entries * 4 * 8192 * 20, bytes_accessed=2_000_000, transcendentals=entries * 32768
        ),
    )(dev, slot, sep, points, radius, load, split_out, turn, tilt)


def per_device(
    coeffs, degree, material, split_coeffs, split_material, separation, reader_dev, reader_slot
):
    drops, fields, degrees, width = coeffs.shape
    row_count, col_count = lax.axis_size("row"), lax.axis_size("col")
    devices = row_count * col_count
    tables = spectral_tables(degrees)
    legendre, fourier, weight, sine, cosine, lon = tables
    nlat, nlon = degrees, 2 * degrees

    lat_points = range(nlat // 4, nlat, nlat // 2)
    lon_points = range(0, nlon, nlon // 2)
    spots = [(j, k) for j in lat_points for k in lon_points]
    normals = [
        (
            float(sine[j] * math.cos(lon[k])),
            float(sine[j] * math.sin(lon[k])),
            float(cosine[j]),
        )
        for j, k in spots
    ]
    order = np.arange(width) % degrees
    basis = jnp.asarray(
        np.stack([legendre[order, j, :].T * fourier[:, k][None, :] for j, k in spots]), F32
    )
    traction_coeffs, radius, load, split_out, points = spectral(
        coeffs, degree, material, split_coeffs, split_material, basis, tables, devices
    )
    point_count = len(spots)
    columns = -(-3 * drops * point_count // LANES) * LANES
    velocity, split_traction = near(
        reader_dev.T, reader_slot.T, jnp.transpose(separation, (0, 2, 1)),
        points.reshape(devices * drops, LANES), radius, load, split_out,
        tables, normals, devices, columns,
    )
    return traction_coeffs, split_traction, velocity


def solution(mesh):
    both = ("row", "col")
    in_specs = (
        P(both, None, None, None),
        P(both),
        P(both, None),
        P(both, None, None, None),
        P(),
        P(None, both, None),
        P(both, None),
        P(both, None),
    )
    out_specs = (P(both, None, None), P(both, None, None), P(None, both))
    return jax.shard_map(
        per_device, mesh=mesh, in_specs=in_specs, out_specs=out_specs, check_vma=False
    )
```
